256 devices in a mesh: tile: 64 (over z_lo, x, y), pos: 4 (over z_hi, core).
Axes of the slice: x: 4, y: 4, z: 8 (z_hi: 2, z_lo: 4; z = z_hi * 4 + z_lo), core: 2. Of those that a mesh axis runs over, the one named last changes fastest.
Arguments:
- object_tiles: float32 [64, 2, 512, 512], P('tile'), may hold values from -5 to 5
- probe: float32 [2, 256, 256], replicated, may hold values from -6 to 6
- patterns: bfloat16 [2048, 256, 256], P(('tile', 'pos')), may hold values from 0 to 4
- corners: int32 [2048, 2], P(('tile', 'pos')), may hold values from 0 to 511, as said below
- counts: int32 [256], P(('tile', 'pos')), may hold values from 1 to 7, as said below
Outputs:
- refined: float32 [64, 2, 512, 512], P('tile')
The draws below stay inside these ranges and needn't reach their ends.
Inputs may be any that keep to these rules, and one draw needn't show every extreme that they name: `corners`: tile t sits in grid cell (t + 8 + 8 // 2) mod 64 of a row-major grid of 8 tiles a row. A corner row is at most 256 for slots of tiles in the grid's last row, a corner column at most 256 for slots of tiles in the grid's last column, so every crop lies inside the object. The device at tile index t and the one at tile index t + 32 with the same pos index have counts that sum to exactly 8; some device has 7.
All inputs are finite; a program needn't handle non-finite values.
Results may differ from the reference program's by a relative error of at most 0.018.
Values may be sent and summed in bfloat16 or wider, within the bound.
A program may use at most 64 MiB of HBM per device.

```python
import math
import jax
import jax.numpy as jnp
from jax import lax

W = 256
TILE = 512
TILE_COLS = 8
SLOTS = 8
ITERS = 2
TILES = 64
SHARERS = 4
TILE_ROWS = 8
POSITIONS = 2048


def draw_corners(key, part):
    slot_ids = jnp.arange(POSITIONS, dtype=jnp.int32)
    tile_ids = slot_ids // (SLOTS * SHARERS)
    cell_ids = (tile_ids + TILE_COLS + TILE_COLS // 2) % TILES
    first_slot = slot_ids % SLOTS == 0
    last_row = cell_ids // TILE_COLS == TILE_ROWS - 1
    last_col = cell_ids % TILE_COLS == TILE_COLS - 1
    row_limit = jnp.where(last_row, TILE - W + 1, TILE).astype(jnp.int32)
    col_limit = jnp.where(last_col, TILE - W + 1, TILE).astype(jnp.int32)
    row_floor = jnp.where(first_slot & jnp.logical_not(last_row), TILE - W + 1, 0).astype(jnp.int32)
    col_floor = jnp.where(first_slot & jnp.logical_not(last_col), TILE - W + 1, 0).astype(jnp.int32)
    row_key = jax.random.fold_in(key, 11)
    col_key = jax.random.fold_in(key, 12)
    corner_rows = jax.random.randint(row_key, (POSITIONS,), row_floor, row_limit, dtype=jnp.int32)
    corner_cols = jax.random.randint(col_key, (POSITIONS,), col_floor, col_limit, dtype=jnp.int32)
    return jnp.stack([corner_rows, corner_cols], 1)


def draw_counts(key, part):
    lower_half = jax.random.randint(jax.random.fold_in(key, 21), (TILES // 2, SHARERS), 1, SLOTS, dtype=jnp.int32)
    lower_half = lower_half.at[0, 0].set(SLOTS - 1)
    upper_half = SLOTS - lower_half
    return jnp.concatenate([lower_half, upper_half], 0).reshape(TILES * SHARERS).astype(jnp.int32)


def steps_of(rng, dims, cuts, smallest, high):
    gain, own = 1.0, jax.random.fold_in(rng, 6)
    for position, blocks in cuts:
        draws = jnp.exp(jax.random.uniform(jax.random.fold_in(own, position), (blocks,), jnp.float32, smallest / len(cuts), high / len(cuts)))
        gain = gain * jnp.repeat(draws, dims[position] // blocks).reshape([-1 if axis == position else 1 for axis in range(len(dims))])
    return gain


def bell_draw(rng, shape, width, most, split=(), kind=jnp.bfloat16):
    level = steps_of(rng, shape, split, -0.22, 0.18) if split else 1.0
    entries = jax.random.normal(rng, shape, jnp.float32) * width * level
    return jnp.minimum(jnp.maximum(entries, -most), most).astype(kind)


def setup_inputs(seed: int = 0) -> dict:
    splits = jax.random.split(jax.random.key(seed), 6)
    return {
        "object_tiles": bell_draw(splits[0], (TILES, 2, TILE, TILE), 0.7, 5.0, ((0, 64),), jnp.float32),
        "probe": bell_draw(splits[1], (2, W, W), 1.0, 6.0, (), jnp.float32),
        "patterns": jnp.clip(4.0 * jax.random.uniform(splits[2], (POSITIONS, W, W), jnp.float32) ** steps_of(splits[2], (POSITIONS, W, W), ((0, 256),), -0.2, 0.2), 0.0, 4.0).astype(jnp.bfloat16),
        "corners": draw_corners(jax.random.fold_in(splits[5], 71), 0),
        "counts": draw_counts(jax.random.fold_in(splits[5], 71), 0),
    }


LEARNING_RATE = 0.03

def tables(extent):
    counter = jnp.arange(extent, dtype=jnp.int32)
    phases = counter[:, None] * counter[None, :] % extent
    angles = phases.astype(jnp.float32) * (2.0 * math.pi / extent)
    factor = 1.0 / math.sqrt(extent)
    cosine = jnp.cos(angles) * factor
    sine_neg = -jnp.sin(angles) * factor
    forward_right = jnp.concatenate([jnp.concatenate([cosine, sine_neg], 1), jnp.concatenate([-sine_neg, cosine], 1)], 0).astype(jnp.bfloat16)
    forward_left = jnp.concatenate([cosine, sine_neg], 0).astype(jnp.bfloat16)
    backward_right = jnp.concatenate([jnp.concatenate([cosine, -sine_neg], 1), jnp.concatenate([sine_neg, cosine], 1)], 0).astype(jnp.bfloat16)
    backward_left = jnp.concatenate([cosine, -sine_neg], 0).astype(jnp.bfloat16)
    return (forward_right, forward_left, backward_right, backward_left)

def transform(waves, right_table, left_table):
    number, extent = (waves.shape[0], waves.shape[1])
    halfway = jnp.dot(waves.reshape(number * extent, 2 * extent), right_table, preferred_element_type=jnp.float32)
    halfway = lax.optimization_barrier(halfway.reshape(number, extent, 2 * extent).astype(jnp.bfloat16))
    stacked = jnp.einsum('jk,skl->sjl', left_table.astype(jnp.float32), halfway.astype(jnp.float32))
    upper = stacked[:, :extent]
    lower = stacked[:, extent:]
    real_part = upper[:, :, :extent] - lower[:, :, extent:]
    imag_part = upper[:, :, extent:] + lower[:, :, :extent]
    return jnp.concatenate([real_part, imag_part], 2)

def wave_gradient(waves, measured, table_set):
    extent = waves.shape[1]
    spectrum = transform(waves, table_set[0], table_set[1])
    power = spectrum[:, :, :extent] ** 2 + spectrum[:, :, extent:] ** 2
    misfit = power - measured.astype(jnp.float32)
    pushed = (spectrum * jnp.concatenate([misfit, misfit], 2)).astype(jnp.bfloat16)
    return transform(pushed, table_set[2], table_set[3]).astype(jnp.bfloat16)

def exit_waves(probe, crops):
    real_part = probe[0] * crops[:, 0] - probe[1] * crops[:, 1]
    imag_part = probe[0] * crops[:, 1] + probe[1] * crops[:, 0]
    return jnp.concatenate([real_part, imag_part], 2).astype(jnp.bfloat16)

def crop_gradients(probe, wave_grads, alive_mask):
    extent = probe.shape[1]
    real_in = wave_grads[:, :, :extent].astype(jnp.float32)
    imag_in = wave_grads[:, :, extent:].astype(jnp.float32)
    real_part = probe[0] * real_in + probe[1] * imag_in
    imag_part = probe[0] * imag_in - probe[1] * real_in
    return jnp.stack([real_part, imag_part], 1) * alive_mask[:, None, None, None]

def reference(object_tiles, probe, patterns, corners, counts):
    table_set = tables(W)
    rotation = (TILE_COLS + TILE_COLS // 2) % TILES
    cell_tiles = jnp.roll(object_tiles, rotation, axis=0)
    full_object = cell_tiles.reshape(TILE_ROWS, TILE_COLS, 2, TILE, TILE).transpose(2, 0, 3, 1, 4)
    full_object = full_object.reshape(2, TILE_ROWS * TILE, TILE_COLS * TILE)
    slot_ids = jnp.arange(POSITIONS, dtype=jnp.int32)
    device_ids = slot_ids // SLOTS
    tile_ids = device_ids // SHARERS
    cell_ids = (tile_ids + rotation) % TILES
    anchor_rows = (cell_ids // TILE_COLS * TILE + corners[:, 0]).astype(jnp.int32)
    anchor_cols = (cell_ids % TILE_COLS * TILE + corners[:, 1]).astype(jnp.int32)
    live_flags = (slot_ids % SLOTS < counts[device_ids]).astype(jnp.float32)
    for repeat in range(ITERS):
        current = full_object

        def visit_slot(running, scan_item):
            row_at, col_at, measured, alive_flag = scan_item
            anchor = (jnp.zeros((), jnp.int32), row_at, col_at)
            window_crop = lax.dynamic_slice(current, anchor, (2, W, W))
            waves = exit_waves(probe, window_crop[None])
            wave_grads = wave_gradient(waves, measured[None], table_set)
            portion = crop_gradients(probe, wave_grads, alive_flag[None])[0]
            region = lax.dynamic_slice(running, anchor, (2, W, W))
            return (lax.dynamic_update_slice(running, region + portion, anchor), None)
        zeros_image = jnp.zeros(current.shape, jnp.float32)
        grad_image, _ = lax.scan(visit_slot, zeros_image, (anchor_rows, anchor_cols, patterns, live_flags))
        full_object = current - LEARNING_RATE * grad_image
    refined = full_object.reshape(2, TILE_ROWS, TILE, TILE_COLS, TILE).transpose(1, 3, 0, 2, 4)
    refined = refined.reshape(TILES, 2, TILE, TILE)
    return jnp.roll(refined, -rotation, axis=0)
```

```python
import functools
import math

import jax
import jax.numpy as jnp
import numpy as np
from jax import lax
from jax.experimental import pallas as pl
from jax.experimental.pallas import tpu as pltpu
from jax.sharding import PartitionSpec as P

TILE_COLS = 8
ITERS = 2
LEARNING_RATE = 0.03
LANES = 128
SUBLANES = 8
CHUNK = 32


def tables(extent):
    counter = np.arange(extent, dtype=np.int64)
    phases = counter[:, None] * counter[None, :] % extent
    angles = phases.astype(np.float64) * (2.0 * math.pi / extent)
    factor = 1.0 / math.sqrt(extent)
    cosine = np.cos(angles) * factor
    sine_neg = -np.sin(angles) * factor
    first = np.block([[cosine, sine_neg], [-sine_neg, cosine]])
    second = np.block([[cosine, -sine_neg], [sine_neg, cosine]])
    return jnp.asarray(first, jnp.bfloat16), jnp.asarray(second, jnp.bfloat16)


def slots_kernel(
    corners, counts, tile, right, lower, diag, probe, patterns, first, second,
    grad_tile, grad_right, grad_lower, grad_diag,
    image, grad, padded, rolled, wave, half, spectrum,
):
    extent = probe.shape[1]
    edge = tile.shape[1]
    own = edge // LANES
    margin = extent // LANES
    f32 = jnp.float32
    for ch in range(2):
        for b in range(own):
            cols = slice(b * LANES, (b + 1) * LANES)
            image[b, ch, :edge] = tile[ch, :, cols]
            image[b, ch, edge:] = lower[ch, :, cols].astype(f32)
        for b in range(margin):
            cols = slice(b * LANES, (b + 1) * LANES)
            image[own + b, ch, :edge] = right[ch, :, cols].astype(f32)
            image[own + b, ch, edge:] = diag[ch, :, cols].astype(f32)
        for b in range(margin):
            cols = slice(b * LANES, (b + 1) * LANES)
            padded[ch, b, :SUBLANES] = probe[ch, extent - SUBLANES:, cols]
            padded[ch, b, SUBLANES:] = probe[ch, :, cols]
    grad[...] = jnp.zeros_like(grad)

    def slot(g, carry):
        row = corners[g, 0]
        col = corners[g, 1]
        row_off = lax.rem(row, SUBLANES)
        col_off = lax.rem(col, LANES)
        row_at = pl.multiple_of(row - row_off, SUBLANES)
        block = lax.div(col, LANES)
        lane = lax.broadcasted_iota(jnp.int32, (CHUNK, LANES), 1)
        keep = lane >= col_off
        lane8 = lax.broadcasted_iota(jnp.int32, (SUBLANES, LANES), 1)
        sub8 = lax.broadcasted_iota(jnp.int32, (SUBLANES, LANES), 0)
        keep8 = lane8 >= col_off
        stay8 = sub8 >= row_off
        over = pl.multiple_of(row_at + extent, SUBLANES)

        for i in range(0, extent, CHUNK):
            here = slice(i, i + CHUNK)
            shifted = []
            for ch in range(2):
                turned = [
                    pltpu.roll(
                        padded[ch, b, pl.ds(SUBLANES - row_off + i, CHUNK), :], col_off, 1
                    )
                    for b in range(2)
                ]
                shifted.append(
                    (jnp.where(keep, turned[0], turned[1]), jnp.where(keep, turned[1], turned[0]))
                )
                rolled[ch, 0, here] = shifted[ch][0]
                rolled[ch, 1, here] = shifted[ch][1]
            rows = pl.ds(pl.multiple_of(row_at + i, SUBLANES), CHUNK)
            crops = []
            for ch in range(2):
                left = jnp.where(keep, image[block, ch, rows, :], image[block + 2, ch, rows, :])
                mid = image[block + 1, ch, rows, :]
                if i == 0:
                    below = pl.ds(over, SUBLANES)
                    left8 = jnp.where(
                        keep8, image[block, ch, below, :], image[block + 2, ch, below, :]
                    )
                    mid8 = image[block + 1, ch, below, :]
                    left = jnp.concatenate(
                        [jnp.where(stay8, left[:SUBLANES], left8), left[SUBLANES:]], 0
                    )
                    mid = jnp.concatenate(
                        [jnp.where(stay8, mid[:SUBLANES], mid8), mid[SUBLANES:]], 0
                    )
                crops.append((left, mid))
            for b in range(2):
                real = shifted[0][b] * crops[0][b] - shifted[1][b] * crops[1][b]
                imag = shifted[0][b] * crops[1][b] + shifted[1][b] * crops[0][b]
                wave[here, b * LANES:(b + 1) * LANES] = real.astype(jnp.bfloat16)
                wave[here, extent + b * LANES:extent + (b + 1) * LANES] = imag.astype(jnp.bfloat16)

        def rightwards(table):
            result = jnp.dot(wave[...], table[...], preferred_element_type=f32)
            half[:extent] = result[:, :extent].astype(jnp.bfloat16)
            half[extent:] = result[:, extent:].astype(jnp.bfloat16)

        def downwards(table):
            spectrum[...] = jnp.dot(table[...], half[...], preferred_element_type=f32)

        rightwards(first)
        downwards(second)
        for i in range(0, extent, CHUNK):
            here = slice(i, i + CHUNK)
            real = spectrum[here]
            imag = spectrum[extent + i:extent + i + CHUNK]
            misfit = real * real + imag * imag - patterns[g, here].astype(f32)
            wave[here, :extent] = (real * misfit).astype(jnp.bfloat16)
            wave[here, extent:] = (imag * misfit).astype(jnp.bfloat16)
        rightwards(second)
        downwards(first)

        for i in range(0, extent, CHUNK):
            here = slice(i, i + CHUNK)
            rows = pl.ds(pl.multiple_of(row_at + i, SUBLANES), CHUNK)
            for b in range(2):
                cols = slice(b * LANES, (b + 1) * LANES)
                real = spectrum[here, cols]
                imag = spectrum[extent + i:extent + i + CHUNK, cols]
                p_real = rolled[0, b, here]
                p_imag = rolled[1, b, here]
                parts = (p_real * real + p_imag * imag, p_real * imag - p_imag * real)
                for ch in range(2):
                    value = parts[ch]
                    if i == 0:
                        spill = jnp.where(stay8, 0.0, value[:SUBLANES])
                        value = jnp.concatenate(
                            [jnp.where(stay8, value[:SUBLANES], 0.0), value[SUBLANES:]], 0
                        )
                        below = pl.ds(over, SUBLANES)
                        if b == 0:
                            grad[block, ch, below, :] += jnp.where(keep8, spill, 0.0)
                            grad[block + 2, ch, below, :] += jnp.where(keep8, 0.0, spill)
                        else:
                            grad[block + 1, ch, below, :] += spill
                    if b == 0:
                        grad[block, ch, rows, :] += jnp.where(keep, value, 0.0)
                        grad[block + 2, ch, rows, :] += jnp.where(keep, 0.0, value)
                    else:
                        grad[block + 1, ch, rows, :] += value
        return carry

    lax.fori_loop(0, counts[0], slot, 0)

    for ch in range(2):
        for b in range(own):
            cols = slice(b * LANES, (b + 1) * LANES)
            grad_tile[ch, :, cols] = grad[b, ch, :edge].astype(jnp.bfloat16)
            grad_lower[ch, :, cols] = grad[b, ch, edge:].astype(jnp.bfloat16)
        for b in range(margin):
            cols = slice(b * LANES, (b + 1) * LANES)
            grad_right[ch, :, cols] = grad[own + b, ch, :edge].astype(jnp.bfloat16)
            grad_diag[ch, :, cols] = grad[own + b, ch, edge:].astype(jnp.bfloat16)


def slot_gradients(tile, right, lower, diag, probe, patterns, corners, counts, first, second):
    extent = probe.shape[1]
    edge = tile.shape[1]
    total = edge + extent
    blocks = total // LANES
    f32, bf16 = jnp.float32, jnp.bfloat16
    vmem = pl.BlockSpec(memory_space=pltpu.VMEM)
    smem = pl.BlockSpec(memory_space=pltpu.SMEM)
    return pl.pallas_call(
        slots_kernel,
        out_shape=(
            jax.ShapeDtypeStruct((2, edge, edge), bf16),
            jax.ShapeDtypeStruct((2, edge, extent), bf16),
            jax.ShapeDtypeStruct((2, extent, edge), bf16),
            jax.ShapeDtypeStruct((2, extent, extent), bf16),
        ),
        in_specs=[smem, smem] + [vmem] * 8,
        out_specs=(vmem,) * 4,
        scratch_shapes=[
            pltpu.VMEM((blocks, 2, total, LANES), f32),
            pltpu.VMEM((blocks, 2, total, LANES), f32),
            pltpu.VMEM((2, 2, extent + SUBLANES, LANES), f32),
            pltpu.VMEM((2, 2, extent, LANES), f32),
            pltpu.VMEM((extent, 2 * extent), bf16),
            pltpu.VMEM((2 * extent, extent), bf16),
            pltpu.VMEM((2 * extent, extent), f32),
        ],
        compiler_params=pltpu.CompilerParams(vmem_limit_bytes=40 * 1024 * 1024),
        cost_estimate=pl.CostEstimate(
            flops=4 * 4 * 2 * extent**3 * 2, bytes_accessed=8 * 2**20, transcendentals=0
        ),
    )(corners, counts, tile, right, lower, diag, probe, patterns, first, second)


def shifted_by(value, steps):
    count = lax.axis_size("tile")
    return lax.ppermute(value, "tile", [(s, (s + steps) % count) for s in range(count)])


def shards(object_tiles, probe, patterns, corners, counts):
    tile = object_tiles[0]
    extent = probe.shape[1]
    first, second = tables(extent)
    for repeat in range(ITERS):
        short = tile.astype(jnp.bfloat16)
        right = shifted_by(short[:, :, :extent], -1)
        lower = shifted_by(short[:, :extent, :], -TILE_COLS)
        diag = shifted_by(short[:, :extent, :extent], -TILE_COLS - 1)
        grads = slot_gradients(
            tile, right, lower, diag, probe, patterns, corners, counts, first, second
        )
        total, *margins = grads
        total = total.astype(jnp.float32)
        right_in = shifted_by(margins[0], 1).astype(jnp.float32)
        lower_in = shifted_by(margins[1], TILE_COLS).astype(jnp.float32)
        diag_in = shifted_by(margins[2], TILE_COLS + 1).astype(jnp.float32)
        total = total.at[:, :, :extent].add(right_in)
        total = total.at[:, :extent, :].add(lower_in)
        total = total.at[:, :extent, :extent].add(diag_in)
        tile = tile - LEARNING_RATE * lax.psum(total.astype(jnp.bfloat16), "pos").astype(
            jnp.float32
        )
    return tile[None]


def solution(mesh):
    return jax.shard_map(
        shards,
        mesh=mesh,
        in_specs=(
            P("tile", None, None, None),
            P(),
            P(("tile", "pos"), None, None),
            P(("tile", "pos"), None),
            P(("tile", "pos")),
        ),
        out_specs=P("tile", None, None, None),
        check_vma=False,
    )
```

```python
import functools
import math

import jax
import jax.numpy as jnp
import numpy as np
from jax import lax
from jax.experimental import pallas as pl
from jax.experimental.pallas import tpu as pltpu
from jax.sharding import PartitionSpec as P

TILE_COLS = 8
ITERS = 2
LEARNING_RATE = 0.03
LANES = 128
SUBLANES = 8
CHUNK = 32
BAND = 3
RIGHT, LOWER, DIAG, PIECES = 0, 2, 4, 5
MESH = pl.DeviceIdType.MESH


def tables(extent):
    counter = np.arange(extent, dtype=np.int64)
    phases = counter[:, None] * counter[None, :] % extent
    angles = phases.astype(np.float64) * (2.0 * math.pi / extent)
    factor = 1.0 / math.sqrt(extent)
    cosine = np.cos(angles) * factor
    sine_neg = -np.sin(angles) * factor
    first = np.block([[cosine, sine_neg], [-sine_neg, cosine]])
    second = np.block([[cosine, -sine_neg], [sine_neg, cosine]])
    return jnp.asarray(first, jnp.bfloat16), jnp.asarray(second, jnp.bfloat16)


def slots_kernel(
    corners, counts, tile, halo, probe, patterns, first, second,
    grad_blocks,
    image, grad, padded, rolled, wave, half, spectrum,
):
    extent = probe.shape[1]
    edge = tile.shape[1]
    own = edge // LANES
    margin = extent // LANES
    f32 = jnp.float32
    for ch in range(2):
        for b in range(own):
            cols = slice(b * LANES, (b + 1) * LANES)
            image[b, ch, :edge] = tile[ch, :, cols]
            inner = slice(b % margin * LANES, (b % margin + 1) * LANES)
            image[b, ch, edge:] = halo[ch, LOWER + b // margin, :, inner].astype(f32)
        for b in range(margin):
            cols = slice(b * LANES, (b + 1) * LANES)
            for i in range(edge // extent):
                image[own + b, ch, i * extent:(i + 1) * extent] = halo[ch, RIGHT + i, :, cols].astype(f32)
            image[own + b, ch, edge:] = halo[ch, DIAG, :, cols].astype(f32)
            padded[ch, b, :SUBLANES] = probe[ch, extent - SUBLANES:, cols]
            padded[ch, b, SUBLANES:] = probe[ch, :, cols]
    grad[...] = jnp.zeros_like(grad)

    def slot(g, carry):
        row = corners[g, 0]
        col = corners[g, 1]
        row_off = lax.rem(row, SUBLANES)
        col_off = lax.rem(col, LANES)
        row_at = pl.multiple_of(row - row_off, SUBLANES)
        block = lax.div(col, LANES)
        lane = lax.broadcasted_iota(jnp.int32, (CHUNK, LANES), 1)
        keep = lane >= col_off
        lane8 = lax.broadcasted_iota(jnp.int32, (SUBLANES, LANES), 1)
        sub8 = lax.broadcasted_iota(jnp.int32, (SUBLANES, LANES), 0)
        keep8 = lane8 >= col_off
        stay8 = sub8 >= row_off
        over = pl.multiple_of(row_at + extent, SUBLANES)

        for i in range(0, extent, CHUNK):
            here = slice(i, i + CHUNK)
            shifted = []
            for ch in range(2):
                turned = [
                    pltpu.roll(
                        padded[ch, b, pl.ds(SUBLANES - row_off + i, CHUNK), :], col_off, 1
                    )
                    for b in range(2)
                ]
                shifted.append(
                    (jnp.where(keep, turned[0], turned[1]), jnp.where(keep, turned[1], turned[0]))
                )
                rolled[ch, 0, here] = shifted[ch][0]
                rolled[ch, 1, here] = shifted[ch][1]
            rows = pl.ds(pl.multiple_of(row_at + i, SUBLANES), CHUNK)
            crops = []
            for ch in range(2):
                left = jnp.where(keep, image[block, ch, rows, :], image[block + 2, ch, rows, :])
                mid = image[block + 1, ch, rows, :]
                if i == 0:
                    below = pl.ds(over, SUBLANES)
                    left8 = jnp.where(
                        keep8, image[block, ch, below, :], image[block + 2, ch, below, :]
                    )
                    mid8 = image[block + 1, ch, below, :]
                    left = jnp.concatenate(
                        [jnp.where(stay8, left[:SUBLANES], left8), left[SUBLANES:]], 0
                    )
                    mid = jnp.concatenate(
                        [jnp.where(stay8, mid[:SUBLANES], mid8), mid[SUBLANES:]], 0
                    )
                crops.append((left, mid))
            for b in range(2):
                real = shifted[0][b] * crops[0][b] - shifted[1][b] * crops[1][b]
                imag = shifted[0][b] * crops[1][b] + shifted[1][b] * crops[0][b]
                wave[here, b * LANES:(b + 1) * LANES] = real.astype(jnp.bfloat16)
                wave[here, extent + b * LANES:extent + (b + 1) * LANES] = imag.astype(jnp.bfloat16)

        def rightwards(table):
            result = jnp.dot(wave[...], table[...], preferred_element_type=f32)
            half[:extent] = result[:, :extent].astype(jnp.bfloat16)
            half[extent:] = result[:, extent:].astype(jnp.bfloat16)

        def downwards(table):
            spectrum[...] = jnp.dot(table[...], half[...], preferred_element_type=f32)

        rightwards(first)
        downwards(second)
        for i in range(0, extent, CHUNK):
            here = slice(i, i + CHUNK)
            real = spectrum[here]
            imag = spectrum[extent + i:extent + i + CHUNK]
            misfit = real * real + imag * imag - patterns[g, here].astype(f32)
            wave[here, :extent] = (real * misfit).astype(jnp.bfloat16)
            wave[here, extent:] = (imag * misfit).astype(jnp.bfloat16)
        rightwards(second)
        downwards(first)

        for i in range(0, extent, CHUNK):
            here = slice(i, i + CHUNK)
            rows = pl.ds(pl.multiple_of(row_at + i, SUBLANES), CHUNK)
            for b in range(2):
                cols = slice(b * LANES, (b + 1) * LANES)
                real = spectrum[here, cols]
                imag = spectrum[extent + i:extent + i + CHUNK, cols]
                p_real = rolled[0, b, here]
                p_imag = rolled[1, b, here]
                parts = (p_real * real + p_imag * imag, p_real * imag - p_imag * real)
                for ch in range(2):
                    value = parts[ch]
                    if i == 0:
                        spill = jnp.where(stay8, 0.0, value[:SUBLANES])
                        value = jnp.concatenate(
                            [jnp.where(stay8, value[:SUBLANES], 0.0), value[SUBLANES:]], 0
                        )
                        below = pl.ds(over, SUBLANES)
                        if b == 0:
                            grad[block, ch, below, :] += jnp.where(keep8, spill, 0.0)
                            grad[block + 2, ch, below, :] += jnp.where(keep8, 0.0, spill)
                        else:
                            grad[block + 1, ch, below, :] += spill
                    if b == 0:
                        grad[block, ch, rows, :] += jnp.where(keep, value, 0.0)
                        grad[block + 2, ch, rows, :] += jnp.where(keep, 0.0, value)
                    else:
                        grad[block + 1, ch, rows, :] += value
        return carry

    lax.fori_loop(0, counts[0], slot, 0)

    for ch in range(2):
        for i in range(BAND):
            rows = slice(i * extent, (i + 1) * extent)
            for b in range(BAND * margin):
                cols = slice(b % margin * LANES, (b % margin + 1) * LANES)
                grad_blocks[ch, i * BAND + b // margin, :, cols] = grad[b, ch, rows].astype(
                    jnp.bfloat16
                )


def slot_gradients(tile, halo, probe, patterns, corners, counts, first, second):
    extent = probe.shape[1]
    edge = tile.shape[1]
    total = edge + extent
    blocks = total // LANES
    f32, bf16 = jnp.float32, jnp.bfloat16
    vmem = pl.BlockSpec(memory_space=pltpu.VMEM)
    smem = pl.BlockSpec(memory_space=pltpu.SMEM)
    return pl.pallas_call(
        slots_kernel,
        out_shape=jax.ShapeDtypeStruct((2, BAND * BAND, extent, extent), bf16),
        in_specs=[smem, smem] + [vmem] * 6,
        out_specs=vmem,
        scratch_shapes=[
            pltpu.VMEM((blocks, 2, total, LANES), f32),
            pltpu.VMEM((blocks, 2, total, LANES), f32),
            pltpu.VMEM((2, 2, extent + SUBLANES, LANES), f32),
            pltpu.VMEM((2, 2, extent, LANES), f32),
            pltpu.VMEM((extent, 2 * extent), bf16),
            pltpu.VMEM((2 * extent, extent), bf16),
            pltpu.VMEM((2 * extent, extent), f32),
        ],
        compiler_params=pltpu.CompilerParams(vmem_limit_bytes=40 * 1024 * 1024),
        cost_estimate=pl.CostEstimate(
            flops=4 * 4 * 2 * extent**3 * 2, bytes_accessed=8 * 2**20, transcendentals=0
        ),
    )(corners, counts, tile, halo, probe, patterns, first, second)


class Place:
    def __init__(self):
        self.tiles = lax.axis_size("tile")
        self.chips = self.tiles * (lax.axis_size("pos") // 2)
        pos = lax.axis_index("pos")
        self.core = lax.rem(pos, 2)
        self.other = 1 - self.core
        self.flat = lax.div(pos, 2) * self.tiles + lax.axis_index("tile")

    def device(self, steps, core):
        flat = lax.rem(self.flat + steps + self.chips, self.chips)
        return lax.rem(flat, self.tiles), lax.div(flat, self.tiles) * 2 + core

    def sibling(self):
        return self.device(0, self.other)

    def chip(self, steps):
        return self.device(steps, self.core)


def greet(devices):
    barrier = pltpu.get_barrier_semaphore()
    for device in devices:
        pl.semaphore_signal(barrier, inc=1, device_id=device, device_id_type=MESH)
    pl.semaphore_wait(barrier, len(devices))


def halo_targets(i, j):
    targets = []
    if j == 0:
        targets.append((RIGHT + i, -1))
    if i == 0:
        targets.append((LOWER + j, -TILE_COLS))
    if i == 0 and j == 0:
        targets.append((DIAG, -TILE_COLS - 1))
    return targets


def remote(source, target, sems, at, device):
    return pltpu.make_async_remote_copy(
        src_ref=source,
        dst_ref=target,
        send_sem=sems.at[0, at],
        recv_sem=sems.at[1, at],
        device_id=device,
        device_id_type=MESH,
    )


def block_of(ref, channel, i, j, extent):
    return ref.at[channel, i * extent:(i + 1) * extent, j * extent:(j + 1) * extent]


def first_halo_kernel(tile, halo, outgoing, halo_sems, pass_sems):
    place = Place()
    extent = outgoing.shape[-1]
    core = place.core
    greet(
        [place.sibling()]
        + [place.chip(sign * s) for s in (1, TILE_COLS, TILE_COLS + 1) for sign in (1, -1)]
    )
    copies = {}
    for i, j in ((0, 0), (1, 0), (0, 1)):
        outgoing[2 * i + j] = block_of(tile, core, i, j, extent)[...].astype(jnp.bfloat16)
        for piece, steps in halo_targets(i, j):
            copies[piece] = remote(
                outgoing.at[2 * i + j], halo.at[core, piece], halo_sems, piece, place.chip(steps)
            )
            copies[piece].start()
    finish_halo(place, halo, copies, pass_sems)


def finish_halo(place, halo, copies, pass_sems):
    passes = []
    for piece, copy in copies.items():
        copy.wait_recv()
        mine = halo.at[place.core, piece]
        passes.append(remote(mine, mine, pass_sems, piece, place.sibling()))
        passes[-1].start()
    for copy in passes:
        copy.wait()
    for copy in copies.values():
        copy.wait_send()


def reduce_kernel(
    last, grads, tile, refined, *rest,
):
    (halo, outgoing, halo_sems, pass_sems) = rest[:4] if not last else (None,) * 4
    (pair, edges, edges_in, sums, sums_in, totals, totals_in,
     pair_sems, edge_sems, sum_sems, total_sems) = rest[0 if last else 4:]
    place = Place()
    extent = grads.shape[-1]
    core, other = place.core, place.other
    f32, bf16 = jnp.float32, jnp.bfloat16
    across = place.tiles
    greet(
        [place.sibling(), place.chip(across)]
        + [place.chip(sign * s) for s in (1, TILE_COLS, TILE_COLS + 1) for sign in (1, -1)]
    )
    margins = {5: (1, 1), 7: (3, TILE_COLS), 2: (0, 1), 8: (4, TILE_COLS + 1), 6: (2, TILE_COLS)}
    order = ((1, 1), (1, 0), (0, 0), (0, 1))
    needs = {(1, 1): (), (1, 0): (1,), (0, 0): (0, 2, 4), (0, 1): (3,)}
    pair_copies = {}
    for k in [4, *margins, 3, 0, 1]:
        pair_copies[k] = remote(grads.at[other, k], pair.at[k], pair_sems, k, place.sibling())
        pair_copies[k].start()
    edge_copies = {}
    sum_copies = {}

    def send_sum(i, j):
        k = BAND * i + j
        at = 2 * i + j
        pair_copies[k].wait_recv()
        value = grads[core, k].astype(f32) + pair[k].astype(f32)
        for m in needs[i, j]:
            edge_copies[m].wait_recv()
            value = value + edges_in[m].astype(f32)
        sums[at] = value.astype(bf16)
        sum_copies[at] = remote(sums.at[at], sums_in.at[at], sum_sems, at, place.chip(across))
        sum_copies[at].start()

    send_sum(1, 1)
    for k, (m, steps) in margins.items():
        pair_copies[k].wait_recv()
        edges[m] = (grads[core, k].astype(f32) + pair[k].astype(f32)).astype(bf16)
        edge_copies[m] = remote(edges.at[m], edges_in.at[m], edge_sems, m, place.chip(steps))
        edge_copies[m].start()
    for i, j in order[1:]:
        send_sum(i, j)

    total_copies = {}
    halo_copies = {}
    for i, j in order:
        at = 2 * i + j
        sum_copies[at].wait_recv()
        total = (sums[at].astype(f32) + sums_in[at].astype(f32)).astype(bf16)
        totals[at] = total
        total_copies[at] = remote(
            totals.at[at], totals_in.at[at], total_sems, at, place.sibling()
        )
        total_copies[at].start()
        fresh = block_of(tile, core, i, j, extent)[...] - LEARNING_RATE * total.astype(f32)
        block_of(refined, core, i, j, extent)[...] = fresh
        if not last and (i, j) != (1, 1):
            outgoing[at] = fresh.astype(bf16)
            for piece, steps in halo_targets(i, j):
                halo_copies[piece] = remote(
                    outgoing.at[at], halo.at[core, piece], halo_sems, piece, place.chip(steps)
                )
                halo_copies[piece].start()
    for i, j in order:
        at = 2 * i + j
        total_copies[at].wait_recv()
        block_of(refined, other, i, j, extent)[...] = block_of(tile, other, i, j, extent)[
            ...
        ] - LEARNING_RATE * totals_in[at].astype(f32)
    if not last:
        finish_halo(place, halo, halo_copies, pass_sems)
    for group in (pair_copies, edge_copies, sum_copies, total_copies):
        for copy in group.values():
            copy.wait_send()


def sems(count):
    return pltpu.SemaphoreType.DMA((2, count))


def first_halo(tile, extent):
    vmem = pl.BlockSpec(memory_space=pltpu.VMEM)
    return pl.pallas_call(
        first_halo_kernel,
        out_shape=jax.ShapeDtypeStruct((2, PIECES, extent, extent), jnp.bfloat16),
        in_specs=[vmem],
        out_specs=vmem,
        scratch_shapes=[
            pltpu.VMEM((4, extent, extent), jnp.bfloat16),
            sems(PIECES),
            sems(PIECES),
        ],
        compiler_params=pltpu.CompilerParams(
            collective_id=0, has_side_effects=True, vmem_limit_bytes=40 * 1024 * 1024
        ),
    )(tile)


def reduce_and_update(grads, tile, last):
    extent = grads.shape[-1]
    vmem = pl.BlockSpec(memory_space=pltpu.VMEM)

    def blocks(count):
        return pltpu.VMEM((count, extent, extent), jnp.bfloat16)

    shapes = [jax.ShapeDtypeStruct(tile.shape, tile.dtype)]
    scratch = []
    if not last:
        shapes.append(jax.ShapeDtypeStruct((2, PIECES, extent, extent), jnp.bfloat16))
        scratch += [blocks(4), sems(PIECES), sems(PIECES)]
    scratch += [blocks(BAND * BAND), blocks(PIECES), blocks(PIECES), blocks(4), blocks(4)]
    scratch += [blocks(4), blocks(4), sems(BAND * BAND), sems(PIECES), sems(4), sems(4)]
    return pl.pallas_call(
        functools.partial(reduce_kernel, last),
        out_shape=tuple(shapes),
        in_specs=[vmem, vmem],
        out_specs=(vmem,) * len(shapes),
        scratch_shapes=scratch,
        compiler_params=pltpu.CompilerParams(
            collective_id=2 if last else 1,
            has_side_effects=True,
            vmem_limit_bytes=40 * 1024 * 1024,
        ),
    )(grads, tile)


def shards(object_tiles, probe, patterns, corners, counts):
    tile = object_tiles[0]
    extent = probe.shape[1]
    first, second = tables(extent)
    halo = first_halo(tile, extent)
    for repeat in range(ITERS):
        grads = slot_gradients(tile, halo, probe, patterns, corners, counts, first, second)
        tile, *rest = reduce_and_update(grads, tile, repeat == ITERS - 1)
        if rest:
            halo = rest[0]
    return tile[None]


def solution(mesh):
    return jax.shard_map(
        shards,
        mesh=mesh,
        in_specs=(
            P("tile", None, None, None),
            P(),
            P(("tile", "pos"), None, None),
            P(("tile", "pos"), None),
            P(("tile", "pos")),
        ),
        out_specs=P("tile", None, None, None),
        check_vma=False,
    )
```

```python
import functools
import math

import jax
import jax.numpy as jnp
import numpy as np
from jax import lax
from jax.experimental import pallas as pl
from jax.experimental.pallas import tpu as pltpu
from jax.sharding import PartitionSpec as P

TILE_COLS = 8
ITERS = 2
LEARNING_RATE = 0.03
LANES = 128
SUBLANES = 8
CHUNK = 32
BAND = 3
RIGHT, LOWER, DIAG, PIECES = 0, 2, 4, 5
PLANE = 16
MESH = pl.DeviceIdType.MESH


def tables(extent):
    counter = np.arange(extent, dtype=np.int64)
    phases = counter[:, None] * counter[None, :] % extent
    angles = phases.astype(np.float64) * (2.0 * math.pi / extent)
    factor = 1.0 / math.sqrt(extent)
    cosine = np.cos(angles) * factor
    sine_neg = -np.sin(angles) * factor
    first = np.block([[cosine, sine_neg], [-sine_neg, cosine]])
    second = np.block([[cosine, -sine_neg], [sine_neg, cosine]])
    return jnp.asarray(first, jnp.bfloat16), jnp.asarray(second, jnp.bfloat16)


def slots_kernel(
    corners, counts, tile, halo, probe, patterns, first, second,
    grad_blocks,
    image, grad, padded, rolled, wave, half, spectrum,
):
    extent = probe.shape[1]
    edge = tile.shape[1]
    own = edge // LANES
    margin = extent // LANES
    f32 = jnp.float32
    for ch in range(2):
        for b in range(own):
            cols = slice(b * LANES, (b + 1) * LANES)
            image[b, ch, :edge] = tile[ch, :, cols]
            inner = slice(b % margin * LANES, (b % margin + 1) * LANES)
            image[b, ch, edge:] = halo[ch, LOWER + b // margin, :, inner].astype(f32)
        for b in range(margin):
            cols = slice(b * LANES, (b + 1) * LANES)
            for i in range(edge // extent):
                image[own + b, ch, i * extent:(i + 1) * extent] = halo[ch, RIGHT + i, :, cols].astype(f32)
            image[own + b, ch, edge:] = halo[ch, DIAG, :, cols].astype(f32)
            padded[ch, b, :SUBLANES] = probe[ch, extent - SUBLANES:, cols]
            padded[ch, b, SUBLANES:] = probe[ch, :, cols]
    grad[...] = jnp.zeros_like(grad)

    def slot(g, carry):
        row = corners[g, 0]
        col = corners[g, 1]
        row_off = lax.rem(row, SUBLANES)
        col_off = lax.rem(col, LANES)
        row_at = pl.multiple_of(row - row_off, SUBLANES)
        block = lax.div(col, LANES)
        lane = lax.broadcasted_iota(jnp.int32, (CHUNK, LANES), 1)
        keep = lane >= col_off
        lane8 = lax.broadcasted_iota(jnp.int32, (SUBLANES, LANES), 1)
        sub8 = lax.broadcasted_iota(jnp.int32, (SUBLANES, LANES), 0)
        keep8 = lane8 >= col_off
        stay8 = sub8 >= row_off
        over = pl.multiple_of(row_at + extent, SUBLANES)

        for i in range(0, extent, CHUNK):
            here = slice(i, i + CHUNK)
            shifted = []
            for ch in range(2):
                turned = [
                    pltpu.roll(
                        padded[ch, b, pl.ds(SUBLANES - row_off + i, CHUNK), :], col_off, 1
                    )
                    for b in range(2)
                ]
                shifted.append(
                    (jnp.where(keep, turned[0], turned[1]), jnp.where(keep, turned[1], turned[0]))
                )
                rolled[ch, 0, here] = shifted[ch][0]
                rolled[ch, 1, here] = shifted[ch][1]
            rows = pl.ds(pl.multiple_of(row_at + i, SUBLANES), CHUNK)
            crops = []
            for ch in range(2):
                left = jnp.where(keep, image[block, ch, rows, :], image[block + 2, ch, rows, :])
                mid = image[block + 1, ch, rows, :]
                if i == 0:
                    below = pl.ds(over, SUBLANES)
                    left8 = jnp.where(
                        keep8, image[block, ch, below, :], image[block + 2, ch, below, :]
                    )
                    mid8 = image[block + 1, ch, below, :]
                    left = jnp.concatenate(
                        [jnp.where(stay8, left[:SUBLANES], left8), left[SUBLANES:]], 0
                    )
                    mid = jnp.concatenate(
                        [jnp.where(stay8, mid[:SUBLANES], mid8), mid[SUBLANES:]], 0
                    )
                crops.append((left, mid))
            for b in range(2):
                real = shifted[0][b] * crops[0][b] - shifted[1][b] * crops[1][b]
                imag = shifted[0][b] * crops[1][b] + shifted[1][b] * crops[0][b]
                wave[here, b * LANES:(b + 1) * LANES] = real.astype(jnp.bfloat16)
                wave[here, extent + b * LANES:extent + (b + 1) * LANES] = imag.astype(jnp.bfloat16)

        def rightwards(table):
            result = jnp.dot(wave[...], table[...], preferred_element_type=f32)
            half[:extent] = result[:, :extent].astype(jnp.bfloat16)
            half[extent:] = result[:, extent:].astype(jnp.bfloat16)

        def downwards(table):
            spectrum[...] = jnp.dot(table[...], half[...], preferred_element_type=f32)

        rightwards(first)
        downwards(second)
        for i in range(0, extent, CHUNK):
            here = slice(i, i + CHUNK)
            real = spectrum[here]
            imag = spectrum[extent + i:extent + i + CHUNK]
            misfit = real * real + imag * imag - patterns[g, here].astype(f32)
            wave[here, :extent] = (real * misfit).astype(jnp.bfloat16)
            wave[here, extent:] = (imag * misfit).astype(jnp.bfloat16)
        rightwards(second)
        downwards(first)

        for i in range(0, extent, CHUNK):
            here = slice(i, i + CHUNK)
            rows = pl.ds(pl.multiple_of(row_at + i, SUBLANES), CHUNK)
            for b in range(2):
                cols = slice(b * LANES, (b + 1) * LANES)
                real = spectrum[here, cols]
                imag = spectrum[extent + i:extent + i + CHUNK, cols]
                p_real = rolled[0, b, here]
                p_imag = rolled[1, b, here]
                parts = (p_real * real + p_imag * imag, p_real * imag - p_imag * real)
                for ch in range(2):
                    value = parts[ch]
                    if i == 0:
                        spill = jnp.where(stay8, 0.0, value[:SUBLANES])
                        value = jnp.concatenate(
                            [jnp.where(stay8, value[:SUBLANES], 0.0), value[SUBLANES:]], 0
                        )
                        below = pl.ds(over, SUBLANES)
                        if b == 0:
                            grad[block, ch, below, :] += jnp.where(keep8, spill, 0.0)
                            grad[block + 2, ch, below, :] += jnp.where(keep8, 0.0, spill)
                        else:
                            grad[block + 1, ch, below, :] += spill
                    if b == 0:
                        grad[block, ch, rows, :] += jnp.where(keep, value, 0.0)
                        grad[block + 2, ch, rows, :] += jnp.where(keep, 0.0, value)
                    else:
                        grad[block + 1, ch, rows, :] += value
        return carry

    lax.fori_loop(0, counts[0], slot, 0)

    for ch in range(2):
        for i in range(BAND):
            rows = slice(i * extent, (i + 1) * extent)
            for b in range(BAND * margin):
                cols = slice(b % margin * LANES, (b % margin + 1) * LANES)
                grad_blocks[ch, i * BAND + b // margin, :, cols] = grad[b, ch, rows].astype(
                    jnp.bfloat16
                )


def slot_gradients(tile, halo, probe, patterns, corners, counts, first, second):
    extent = probe.shape[1]
    edge = tile.shape[1]
    total = edge + extent
    blocks = total // LANES
    f32, bf16 = jnp.float32, jnp.bfloat16
    vmem = pl.BlockSpec(memory_space=pltpu.VMEM)
    smem = pl.BlockSpec(memory_space=pltpu.SMEM)
    return pl.pallas_call(
        slots_kernel,
        out_shape=jax.ShapeDtypeStruct((2, BAND * BAND, extent, extent), bf16),
        in_specs=[smem, smem] + [vmem] * 6,
        out_specs=vmem,
        scratch_shapes=[
            pltpu.VMEM((blocks, 2, total, LANES), f32),
            pltpu.VMEM((blocks, 2, total, LANES), f32),
            pltpu.VMEM((2, 2, extent + SUBLANES, LANES), f32),
            pltpu.VMEM((2, 2, extent, LANES), f32),
            pltpu.VMEM((extent, 2 * extent), bf16),
            pltpu.VMEM((2 * extent, extent), bf16),
            pltpu.VMEM((2 * extent, extent), f32),
        ],
        compiler_params=pltpu.CompilerParams(vmem_limit_bytes=40 * 1024 * 1024),
        cost_estimate=pl.CostEstimate(
            flops=4 * 4 * 2 * extent**3 * 2, bytes_accessed=8 * 2**20, transcendentals=0
        ),
    )(corners, counts, tile, halo, probe, patterns, first, second)


class Place:
    def __init__(self):
        self.tiles = lax.axis_size("tile")
        self.chips = self.tiles * (lax.axis_size("pos") // 2)
        pos = lax.axis_index("pos")
        self.core = lax.rem(pos, 2)
        self.other = 1 - self.core
        self.flat = lax.div(pos, 2) * self.tiles + lax.axis_index("tile")
        self.local = lax.rem(self.flat, PLANE)

    def at(self, flat, core):
        return lax.rem(flat, self.tiles), lax.div(flat, self.tiles) * 2 + core

    def device(self, steps, core):
        return self.at(lax.rem(self.flat + steps + self.chips, self.chips), core)

    def sibling(self):
        return self.device(0, self.other)

    def chip(self, steps):
        return self.device(steps, self.core)

    def in_plane(self, steps):
        local = lax.rem(self.local + steps + PLANE, PLANE)
        return self.at(self.flat - self.local + local, self.core)

    def leaves(self, steps):
        ends = self.local + steps
        return jnp.logical_and(self.core == 1, jnp.logical_or(ends < 0, ends >= PLANE))


def greet(place, extra=()):
    devices = [place.sibling(), place.chip(PLANE), place.chip(-PLANE), *extra]
    for steps in (1, TILE_COLS, TILE_COLS + 1):
        for sign in (1, -1):
            devices += [place.chip(sign * steps), place.in_plane(sign * steps)]
    barrier = pltpu.get_barrier_semaphore()
    for device in devices:
        pl.semaphore_signal(barrier, inc=1, device_id=device, device_id_type=MESH)
    pl.semaphore_wait(barrier, len(devices))


def halo_targets(i, j):
    targets = []
    if j == 0:
        targets.append((RIGHT + i, -1))
    if i == 0:
        targets.append((LOWER + j, -TILE_COLS))
    if i == 0 and j == 0:
        targets.append((DIAG, -TILE_COLS - 1))
    return targets


def remote(source, target, sems, at, device):
    return pltpu.make_async_remote_copy(
        src_ref=source,
        dst_ref=target,
        send_sem=sems.at[0, at],
        recv_sem=sems.at[1, at],
        device_id=device,
        device_id_type=MESH,
    )


class Routed:
    def __init__(self, place, steps, source, target, via, at, direct_sems, via_sems, on_sems):
        self.direct = remote(source, target, direct_sems, at, place.chip(steps))
        self.away = remote(source, via.at[at], via_sems, at, place.in_plane(steps))
        self.onward = pltpu.make_async_remote_copy(
            src_ref=via.at[at],
            dst_ref=target,
            send_sem=on_sems.at[at],
            recv_sem=direct_sems.at[1, at],
            device_id=place.chip(PLANE if steps > 0 else -PLANE),
            device_id_type=MESH,
        )
        self.leaves = place.leaves(steps)
        self.hands_on = place.leaves(-steps)

    def start(self):
        @pl.when(self.leaves)
        def _():
            self.away.start()

        @pl.when(jnp.logical_not(self.leaves))
        def _():
            self.direct.start()

    def hand_on(self):
        @pl.when(self.hands_on)
        def _():
            self.away.wait_recv()
            self.onward.start()

    def wait_recv(self):
        self.direct.wait_recv()

    def wait_send(self):
        @pl.when(self.leaves)
        def _():
            self.away.wait_send()

        @pl.when(jnp.logical_not(self.leaves))
        def _():
            self.direct.wait_send()

        @pl.when(self.hands_on)
        def _():
            self.onward.wait_send()


def block_of(ref, channel, i, j, extent):
    return ref.at[channel, i * extent:(i + 1) * extent, j * extent:(j + 1) * extent]


HALO_ORDER = (RIGHT + 1, RIGHT, LOWER, DIAG, LOWER + 1)


def send_halos(place, copies, i, j, outgoing, halo, via, halo_sems, via_sems, on_sems):
    for piece, steps in halo_targets(i, j):
        copies[piece] = Routed(
            place, steps, outgoing.at[2 * i + j], halo.at[place.core, piece], via, piece,
            halo_sems, via_sems, on_sems,
        )
        copies[piece].start()


def pass_halos(place, halo, copies, pass_sems):
    passes = []
    for piece in HALO_ORDER:
        copies[piece].wait_recv()
        mine = halo.at[place.core, piece]
        passes.append(remote(mine, mine, pass_sems, piece, place.sibling()))
        passes[-1].start()
    for copy in passes:
        copy.wait()
    for copy in copies.values():
        copy.wait_send()


def first_halo_kernel(tile, halo, outgoing, via, halo_sems, via_sems, on_sems, pass_sems):
    place = Place()
    extent = outgoing.shape[-1]
    greet(place)
    copies = {}
    for i, j in ((1, 0), (0, 0), (0, 1)):
        outgoing[2 * i + j] = block_of(tile, place.core, i, j, extent)[...].astype(jnp.bfloat16)
        send_halos(place, copies, i, j, outgoing, halo, via, halo_sems, via_sems, on_sems)
    for piece in HALO_ORDER:
        copies[piece].hand_on()
    pass_halos(place, halo, copies, pass_sems)


def reduce_kernel(last, grads, tile, refined, *rest):
    if not last:
        halo, outgoing, halo_via, halo_sems, halo_via_sems, halo_on_sems, pass_sems = rest[:7]
        rest = rest[7:]
    (pair, edges, edges_in, edges_via, sums, sums_in, totals, totals_in,
     pair_sems, edge_sems, edge_via_sems, edge_on_sems, sum_sems, total_sems) = rest
    place = Place()
    extent = grads.shape[-1]
    core, other = place.core, place.other
    f32, bf16 = jnp.float32, jnp.bfloat16
    across = place.tiles
    greet(place, (place.chip(across),))
    margins = {5: (1, 1), 7: (3, TILE_COLS), 2: (0, 1), 8: (4, TILE_COLS + 1), 6: (2, TILE_COLS)}
    order = ((1, 1), (1, 0), (0, 0), (0, 1))
    needs = {(1, 1): (), (1, 0): (1,), (0, 0): (0, 2, 4), (0, 1): (3,)}
    pair_copies = {}
    for k in [4, *margins, 3, 0, 1]:
        pair_copies[k] = remote(grads.at[other, k], pair.at[k], pair_sems, k, place.sibling())
        pair_copies[k].start()
    edge_copies = {}
    sum_copies = {}

    def send_sum(i, j):
        k = BAND * i + j
        at = 2 * i + j
        pair_copies[k].wait_recv()
        value = grads[core, k].astype(f32) + pair[k].astype(f32)
        for m in needs[i, j]:
            edge_copies[m].wait_recv()
            value = value + edges_in[m].astype(f32)
        sums[at] = value.astype(bf16)
        sum_copies[at] = remote(sums.at[at], sums_in.at[at], sum_sems, at, place.chip(across))
        sum_copies[at].start()

    send_sum(1, 1)
    for k, (m, steps) in margins.items():
        pair_copies[k].wait_recv()
        edges[m] = (grads[core, k].astype(f32) + pair[k].astype(f32)).astype(bf16)
        edge_copies[m] = Routed(
            place, steps, edges.at[m], edges_in.at[m], edges_via, m,
            edge_sems, edge_via_sems, edge_on_sems,
        )
        edge_copies[m].start()
    edge_copies[1].hand_on()
    send_sum(1, 0)
    for m in (3, 0, 4, 2):
        edge_copies[m].hand_on()
    send_sum(0, 0)
    send_sum(0, 1)

    total_copies = {}
    halo_copies = {}
    for i, j in order:
        at = 2 * i + j
        sum_copies[at].wait_recv()
        total = (sums[at].astype(f32) + sums_in[at].astype(f32)).astype(bf16)
        totals[at] = total
        total_copies[at] = remote(
            totals.at[at], totals_in.at[at], total_sems, at, place.sibling()
        )
        total_copies[at].start()
        fresh = block_of(tile, core, i, j, extent)[...] - LEARNING_RATE * total.astype(f32)
        block_of(refined, core, i, j, extent)[...] = fresh
        if not last and (i, j) != (1, 1):
            outgoing[at] = fresh.astype(bf16)
            send_halos(
                place, halo_copies, i, j, outgoing, halo, halo_via,
                halo_sems, halo_via_sems, halo_on_sems,
            )
            if (i, j) == (0, 0):
                halo_copies[RIGHT + 1].hand_on()
    if not last:
        for piece in HALO_ORDER[1:]:
            halo_copies[piece].hand_on()
    for i, j in order:
        at = 2 * i + j
        total_copies[at].wait_recv()
        block_of(refined, other, i, j, extent)[...] = block_of(tile, other, i, j, extent)[
            ...
        ] - LEARNING_RATE * totals_in[at].astype(f32)
    if not last:
        pass_halos(place, halo, halo_copies, pass_sems)
    for group in (pair_copies, edge_copies, sum_copies, total_copies):
        for copy in group.values():
            copy.wait_send()


def sems(count):
    return pltpu.SemaphoreType.DMA((2, count))


def first_halo(tile, extent):
    vmem = pl.BlockSpec(memory_space=pltpu.VMEM)
    return pl.pallas_call(
        first_halo_kernel,
        out_shape=jax.ShapeDtypeStruct((2, PIECES, extent, extent), jnp.bfloat16),
        in_specs=[vmem],
        out_specs=vmem,
        scratch_shapes=[
            pltpu.VMEM((4, extent, extent), jnp.bfloat16),
            pltpu.VMEM((PIECES, extent, extent), jnp.bfloat16),
            sems(PIECES),
            sems(PIECES),
            pltpu.SemaphoreType.DMA((PIECES,)),
            sems(PIECES),
        ],
        compiler_params=pltpu.CompilerParams(
            collective_id=0, has_side_effects=True, vmem_limit_bytes=40 * 1024 * 1024
        ),
    )(tile)


def reduce_and_update(grads, tile, last):
    extent = grads.shape[-1]
    vmem = pl.BlockSpec(memory_space=pltpu.VMEM)

    def blocks(count):
        return pltpu.VMEM((count, extent, extent), jnp.bfloat16)

    onward = pltpu.SemaphoreType.DMA((PIECES,))
    shapes = [jax.ShapeDtypeStruct(tile.shape, tile.dtype)]
    scratch = []
    if not last:
        shapes.append(jax.ShapeDtypeStruct((2, PIECES, extent, extent), jnp.bfloat16))
        scratch += [blocks(4), blocks(PIECES), sems(PIECES), sems(PIECES), onward, sems(PIECES)]
    scratch += [blocks(BAND * BAND), blocks(PIECES), blocks(PIECES), blocks(PIECES)]
    scratch += [blocks(4), blocks(4), blocks(4), blocks(4)]
    scratch += [sems(BAND * BAND), sems(PIECES), sems(PIECES), onward, sems(4), sems(4)]
    return pl.pallas_call(
        functools.partial(reduce_kernel, last),
        out_shape=tuple(shapes),
        in_specs=[vmem, vmem],
        out_specs=(vmem,) * len(shapes),
        scratch_shapes=scratch,
        compiler_params=pltpu.CompilerParams(
            collective_id=2 if last else 1,
            has_side_effects=True,
            vmem_limit_bytes=40 * 1024 * 1024,
        ),
    )(grads, tile)


def shards(object_tiles, probe, patterns, corners, counts):
    tile = object_tiles[0]
    extent = probe.shape[1]
    first, second = tables(extent)
    halo = first_halo(tile, extent)
    for repeat in range(ITERS):
        grads = slot_gradients(tile, halo, probe, patterns, corners, counts, first, second)
        tile, *rest = reduce_and_update(grads, tile, repeat == ITERS - 1)
        if rest:
            halo = rest[0]
    return tile[None]


def solution(mesh):
    return jax.shard_map(
        shards,
        mesh=mesh,
        in_specs=(
            P("tile", None, None, None),
            P(),
            P(("tile", "pos"), None, None),
            P(("tile", "pos"), None),
            P(("tile", "pos")),
        ),
        out_specs=P("tile", None, None, None),
        check_vma=False,
    )
```

```python
import functools
import math

import jax
import jax.numpy as jnp
import numpy as np
from jax import lax
from jax.experimental import pallas as pl
from jax.experimental.pallas import tpu as pltpu
from jax.sharding import PartitionSpec as P

TILE_COLS = 8
ITERS = 2
LEARNING_RATE = 0.03
LANES = 128
SUBLANES = 8
CHUNK = 32
GROUP = 16
BAND = 3
RIGHT, LOWER, DIAG, PIECES = 0, 2, 4, 5
PLANE = 16
MESH = pl.DeviceIdType.MESH


def tables(extent):
    counter = np.arange(extent, dtype=np.int64)
    phases = counter[:, None] * counter[None, :] % extent
    angles = phases.astype(np.float64) * (2.0 * math.pi / extent)
    factor = 1.0 / math.sqrt(extent)
    cosine = np.cos(angles) * factor
    sine_neg = -np.sin(angles) * factor
    matrices = []
    for parity in range(2):
        c = cosine[:extent // 2, parity::2]
        d = sine_neg[:extent // 2, parity::2]
        matrices.append(np.block([[c, d], [-d, c]]))
    matrices += [matrices[0].T, matrices[1].T]
    rows = np.arange(extent).reshape(2, -1, GROUP).swapaxes(0, 1).reshape(-1)
    matrices += [matrices[at][rows] for at in range(4)]
    order = np.concatenate([counter[0::2], counter[1::2]])
    split = (counter[:, None] == order[None, :]).astype(np.float32)
    return jnp.asarray(np.stack(matrices), jnp.bfloat16), jnp.asarray(
        np.stack([split, split.T]), jnp.bfloat16
    )


def slots_kernel(
    corners, counts, tile, halo, probe, patterns, table,
    grad_blocks,
    image, grad, padded, rolled, wave, half,
):
    extent = probe.shape[1]
    edge = tile.shape[1]
    own = edge // LANES
    margin = extent // LANES
    mid_row = extent // 2
    f32 = jnp.float32
    for ch in range(2):
        for b in range(own):
            cols = slice(b * LANES, (b + 1) * LANES)
            image[b, ch, :edge] = tile[ch, :, cols]
            inner = slice(b % margin * LANES, (b % margin + 1) * LANES)
            image[b, ch, edge:] = halo[ch, LOWER + b // margin, :, inner].astype(f32)
        for b in range(margin):
            cols = slice(b * LANES, (b + 1) * LANES)
            for i in range(edge // extent):
                image[own + b, ch, i * extent:(i + 1) * extent] = halo[ch, RIGHT + i, :, cols].astype(f32)
            image[own + b, ch, edge:] = halo[ch, DIAG, :, cols].astype(f32)
            padded[ch, b, :SUBLANES] = probe[ch, extent - SUBLANES:, cols]
            padded[ch, b, SUBLANES:] = probe[ch, :, cols]
    grad[...] = jnp.zeros_like(grad)

    class Slot:
        def __init__(self, g, lane):
            self.g, self.lane = g, lane
            row, col = corners[g, 0], corners[g, 1]
            self.row_off = lax.rem(row, SUBLANES)
            self.col_off = lax.rem(col, LANES)
            self.row_at = pl.multiple_of(row - self.row_off, SUBLANES)
            self.block = lax.div(col, LANES)
            self.keep = lax.broadcasted_iota(jnp.int32, (CHUNK, LANES), 1) >= self.col_off
            self.keep8 = lax.broadcasted_iota(jnp.int32, (SUBLANES, LANES), 1) >= self.col_off
            self.stay8 = lax.broadcasted_iota(jnp.int32, (SUBLANES, LANES), 0) >= self.row_off
            self.below = pl.ds(pl.multiple_of(self.row_at + extent, SUBLANES), SUBLANES)

        def rows(self, i, number=CHUNK):
            return pl.ds(pl.multiple_of(self.row_at + i, SUBLANES), number)

        def illuminate(self):
            keep, keep8, stay8, block, lane = self.keep, self.keep8, self.stay8, self.block, self.lane
            for i in range(0, extent, CHUNK):
                here = slice(i, i + CHUNK)
                shifted = []
                for ch in range(2):
                    turned = [
                        pltpu.roll(
                            padded[ch, b, pl.ds(SUBLANES - self.row_off + i, CHUNK), :],
                            self.col_off, 1,
                        )
                        for b in range(2)
                    ]
                    shifted.append((
                        jnp.where(keep, turned[0], turned[1]), jnp.where(keep, turned[1], turned[0])
                    ))
                    rolled[lane, ch, 0, here] = shifted[ch][0]
                    rolled[lane, ch, 1, here] = shifted[ch][1]
                rows = self.rows(i)
                crops = []
                for ch in range(2):
                    left = jnp.where(
                        keep, image[block, ch, rows, :], image[block + 2, ch, rows, :]
                    )
                    mid = image[block + 1, ch, rows, :]
                    if i == 0:
                        below = self.below
                        left8 = jnp.where(
                            keep8, image[block, ch, below, :], image[block + 2, ch, below, :]
                        )
                        mid8 = image[block + 1, ch, below, :]
                        left = jnp.concatenate(
                            [jnp.where(stay8, left[:SUBLANES], left8), left[SUBLANES:]], 0
                        )
                        mid = jnp.concatenate(
                            [jnp.where(stay8, mid[:SUBLANES], mid8), mid[SUBLANES:]], 0
                        )
                    crops.append((left, mid))
                real = [
                    shifted[0][b] * crops[0][b] - shifted[1][b] * crops[1][b] for b in range(2)
                ]
                imag = [
                    shifted[0][b] * crops[1][b] + shifted[1][b] * crops[0][b] for b in range(2)
                ]
                wave[lane, 0, here, :LANES] = (real[0] + real[1]).astype(jnp.bfloat16)
                wave[lane, 0, here, LANES:] = (imag[0] + imag[1]).astype(jnp.bfloat16)
                wave[lane, 1, here, :LANES] = (real[0] - real[1]).astype(jnp.bfloat16)
                wave[lane, 1, here, LANES:] = (imag[0] - imag[1]).astype(jnp.bfloat16)

        def along_rows(self):
            lane = self.lane
            for q in range(2):
                freq = jnp.dot(wave[lane, q], table[q], preferred_element_type=f32)
                near, far = freq[:mid_row], freq[mid_row:]
                cols = slice(q * LANES, (q + 1) * LANES)
                for r, value in enumerate((near + far, near - far)):
                    half[lane, r, :mid_row, cols] = value[:, :LANES].astype(jnp.bfloat16)
                    half[lane, r, mid_row:, cols] = value[:, LANES:].astype(jnp.bfloat16)

        def along_columns(self, at, r):
            return jnp.dot(table[at + r], half[self.lane, r], preferred_element_type=f32)

        def push(self):
            lane = self.lane
            for r in range(2):
                freq = self.along_columns(6, r)
                for i in range(0, mid_row, GROUP):
                    here = slice(r * mid_row + i, r * mid_row + i + GROUP)
                    real = freq[2 * i:2 * i + GROUP]
                    imag = freq[2 * i + GROUP:2 * i + 2 * GROUP]
                    misfit = real * real + imag * imag - patterns[self.g, here].astype(f32)
                    real = (real * misfit).astype(jnp.bfloat16)
                    imag = (imag * misfit).astype(jnp.bfloat16)
                    for q in range(2):
                        cols = slice(q * LANES, (q + 1) * LANES)
                        wave[lane, q, here, :LANES] = real[:, cols]
                        wave[lane, q, here, LANES:] = imag[:, cols]

        def back_along_rows(self):
            lane = self.lane
            even = jnp.dot(wave[lane, 0], table[2], preferred_element_type=f32)
            odd = jnp.dot(wave[lane, 1], table[3], preferred_element_type=f32)
            for b, value in enumerate((even + odd, even - odd)):
                cols = slice(b * LANES, (b + 1) * LANES)
                for r in range(2):
                    rows = slice(r * mid_row, (r + 1) * mid_row)
                    half[lane, r, :mid_row, cols] = value[rows, :LANES].astype(jnp.bfloat16)
                    half[lane, r, mid_row:, cols] = value[rows, LANES:].astype(jnp.bfloat16)

        def gather(self):
            keep, keep8, stay8 = self.keep[:GROUP], self.keep8, self.stay8
            block, lane = self.block, self.lane
            even, odd = self.along_columns(4, 0), self.along_columns(4, 1)
            for i in range(0, extent, GROUP):
                here = slice(i, i + GROUP)
                rows = self.rows(i, GROUP)
                both = jnp.add if i < mid_row else jnp.subtract
                at = 2 * (i % mid_row)
                for b in range(2):
                    cols = slice(b * LANES, (b + 1) * LANES)
                    real = both(even[at:at + GROUP, cols], odd[at:at + GROUP, cols])
                    at_imag = slice(at + GROUP, at + 2 * GROUP)
                    imag = both(even[at_imag, cols], odd[at_imag, cols])
                    p_real = rolled[lane, 0, b, here]
                    p_imag = rolled[lane, 1, b, here]
                    parts = (p_real * real + p_imag * imag, p_real * imag - p_imag * real)
                    for ch in range(2):
                        value = parts[ch]
                        if i == 0:
                            spill = jnp.where(stay8, 0.0, value[:SUBLANES])
                            value = jnp.concatenate(
                                [jnp.where(stay8, value[:SUBLANES], 0.0), value[SUBLANES:]], 0
                            )
                            below = self.below
                            if b == 0:
                                grad[block, ch, below, :] += jnp.where(keep8, spill, 0.0)
                                grad[block + 2, ch, below, :] += jnp.where(keep8, 0.0, spill)
                            else:
                                grad[block + 1, ch, below, :] += spill
                        if b == 0:
                            grad[block, ch, rows, :] += jnp.where(keep, value, 0.0)
                            grad[block + 2, ch, rows, :] += jnp.where(keep, 0.0, value)
                        else:
                            grad[block + 1, ch, rows, :] += value

        def stages(self):
            return (
                self.illuminate,
                self.along_rows,
                self.push,
                self.back_along_rows,
                self.gather,
            )

    def pair(p, carry):
        ahead, behind = Slot(2 * p, 0).stages(), Slot(2 * p + 1, 1).stages()
        for a, b in zip(ahead, behind):
            a()
            b()
        return carry

    live = counts[0]
    lax.fori_loop(0, lax.div(live, 2), pair, 0)

    @pl.when(lax.rem(live, 2) == 1)
    def _():
        for stage in Slot(live - 1, 0).stages():
            stage()

    for ch in range(2):
        for i in range(BAND):
            rows = slice(i * extent, (i + 1) * extent)
            for b in range(BAND * margin):
                cols = slice(b % margin * LANES, (b % margin + 1) * LANES)
                grad_blocks[ch, i * BAND + b // margin, :, cols] = grad[b, ch, rows].astype(
                    jnp.bfloat16
                )


def slot_gradients(tile, halo, probe, patterns, corners, counts, table):
    extent = probe.shape[1]
    edge = tile.shape[1]
    total = edge + extent
    blocks = total // LANES
    f32, bf16 = jnp.float32, jnp.bfloat16
    vmem = pl.BlockSpec(memory_space=pltpu.VMEM)
    smem = pl.BlockSpec(memory_space=pltpu.SMEM)
    return pl.pallas_call(
        slots_kernel,
        out_shape=jax.ShapeDtypeStruct((2, BAND * BAND, extent, extent), bf16),
        in_specs=[smem, smem] + [vmem] * 5,
        out_specs=vmem,
        scratch_shapes=[
            pltpu.VMEM((blocks, 2, total, LANES), f32),
            pltpu.VMEM((blocks, 2, total, LANES), f32),
            pltpu.VMEM((2, 2, extent + SUBLANES, LANES), f32),
            pltpu.VMEM((2, 2, 2, extent, LANES), f32),
            pltpu.VMEM((2, 2, extent, extent), bf16),
            pltpu.VMEM((2, 2, extent, extent), bf16),
        ],
        compiler_params=pltpu.CompilerParams(vmem_limit_bytes=40 * 1024 * 1024),
        cost_estimate=pl.CostEstimate(
            flops=4 * 4 * 2 * extent**3 * 2, bytes_accessed=8 * 2**20, transcendentals=0
        ),
    )(corners, counts, tile, halo, probe, patterns, table)


class Place:
    def __init__(self):
        self.tiles = lax.axis_size("tile")
        self.chips = self.tiles * (lax.axis_size("pos") // 2)
        pos = lax.axis_index("pos")
        self.core = lax.rem(pos, 2)
        self.other = 1 - self.core
        self.flat = lax.div(pos, 2) * self.tiles + lax.axis_index("tile")
        self.local = lax.rem(self.flat, PLANE)

    def at(self, flat, core):
        return lax.rem(flat, self.tiles), lax.div(flat, self.tiles) * 2 + core

    def device(self, steps, core):
        return self.at(lax.rem(self.flat + steps + self.chips, self.chips), core)

    def sibling(self):
        return self.device(0, self.other)

    def chip(self, steps):
        return self.device(steps, self.core)

    def in_plane(self, steps):
        local = lax.rem(self.local + steps + PLANE, PLANE)
        return self.at(self.flat - self.local + local, self.core)

    def leaves(self, steps):
        ends = self.local + steps
        return jnp.logical_or(ends < 0, ends >= PLANE)


def greet(place, extra=()):
    devices = [place.sibling(), place.chip(PLANE), place.chip(-PLANE), *extra]
    for sign in (1, -1):
        devices += [place.in_plane(sign)]
        devices += [place.chip(sign * steps) for steps in (1, TILE_COLS, TILE_COLS + 1)]
    barrier = pltpu.get_barrier_semaphore()
    for device in devices:
        pl.semaphore_signal(barrier, inc=1, device_id=device, device_id_type=MESH)
    pl.semaphore_wait(barrier, len(devices))


def halo_targets(i, j):
    targets = []
    if j == 0:
        targets.append((RIGHT + i, -1))
    if i == 0:
        targets.append((LOWER + j, -TILE_COLS))
    if i == 0 and j == 0:
        targets.append((DIAG, -TILE_COLS - 1))
    return targets


def remote(source, target, sems, at, device):
    return pltpu.make_async_remote_copy(
        src_ref=source,
        dst_ref=target,
        send_sem=sems.at[0, at],
        recv_sem=sems.at[1, at],
        device_id=device,
        device_id_type=MESH,
    )


class Routed:
    def __init__(self, place, steps, source, target, via, at, direct_sems, via_sems, on_sems):
        self.direct = remote(source, target, direct_sems, at, place.chip(steps))
        self.away = remote(source, via.at[at], via_sems, at, place.in_plane(steps))
        self.onward = pltpu.make_async_remote_copy(
            src_ref=via.at[at],
            dst_ref=target,
            send_sem=on_sems.at[at],
            recv_sem=direct_sems.at[1, at],
            device_id=place.chip(PLANE if steps > 0 else -PLANE),
            device_id_type=MESH,
        )
        self.leaves = place.leaves(steps)
        self.hands_on = place.leaves(-steps)

    def start(self):
        @pl.when(self.leaves)
        def _():
            self.away.start()

        @pl.when(jnp.logical_not(self.leaves))
        def _():
            self.direct.start()

    def hand_on(self):
        @pl.when(self.hands_on)
        def _():
            self.away.wait_recv()
            self.onward.start()

    def wait_recv(self):
        self.direct.wait_recv()

    def wait_send(self):
        @pl.when(self.leaves)
        def _():
            self.away.wait_send()

        @pl.when(jnp.logical_not(self.leaves))
        def _():
            self.direct.wait_send()

        @pl.when(self.hands_on)
        def _():
            self.onward.wait_send()


def along(place, steps, source, target, via, at, direct_sems, via_sems, on_sems):
    if abs(steps) > 1:
        return remote(source, target, direct_sems, at, place.chip(steps))
    return Routed(place, steps, source, target, via, at, direct_sems, via_sems, on_sems)


def hand_on(copy):
    if isinstance(copy, Routed):
        copy.hand_on()


def block_of(ref, channel, i, j, extent):
    return ref.at[channel, i * extent:(i + 1) * extent, j * extent:(j + 1) * extent]


HALO_ORDER = (RIGHT + 1, RIGHT, LOWER, DIAG, LOWER + 1)


def send_halos(place, copies, i, j, outgoing, halo, via, halo_sems, via_sems, on_sems):
    for piece, steps in halo_targets(i, j):
        copies[piece] = along(
            place, steps, outgoing.at[2 * i + j], halo.at[place.core, piece], via, piece,
            halo_sems, via_sems, on_sems,
        )
        copies[piece].start()


def pass_halos(place, halo, copies, pass_sems):
    passes = []
    for piece in HALO_ORDER:
        copies[piece].wait_recv()
        mine = halo.at[place.core, piece]
        passes.append(remote(mine, mine, pass_sems, piece, place.sibling()))
        passes[-1].start()
    for copy in passes:
        copy.wait()
    for copy in copies.values():
        copy.wait_send()


def first_halo_kernel(
    tile, patterns, split, halo, ordered, outgoing, via, halo_sems, via_sems, on_sems, pass_sems,
):
    place = Place()
    extent = outgoing.shape[-1]
    greet(place)
    copies = {}
    for i, j in ((1, 0), (0, 0), (0, 1)):
        outgoing[2 * i + j] = block_of(tile, place.core, i, j, extent)[...].astype(jnp.bfloat16)
        send_halos(place, copies, i, j, outgoing, halo, via, halo_sems, via_sems, on_sems)

    def reorder(g, carry):
        by_columns = jnp.dot(patterns[g], split[0], preferred_element_type=jnp.float32)
        by_rows = jnp.dot(
            split[1], by_columns.astype(jnp.bfloat16), preferred_element_type=jnp.float32
        )
        ordered[g] = by_rows.astype(jnp.bfloat16)
        return carry

    lax.fori_loop(0, patterns.shape[0], reorder, 0)
    for piece in HALO_ORDER:
        hand_on(copies[piece])
    pass_halos(place, halo, copies, pass_sems)


def reduce_kernel(last, grads, tile, refined, *rest):
    if not last:
        halo, outgoing, halo_via, halo_sems, halo_via_sems, halo_on_sems, pass_sems = rest[:7]
        rest = rest[7:]
    (pair, edges, edges_in, edges_via, sums, sums_in, totals, totals_in,
     pair_sems, edge_sems, edge_via_sems, edge_on_sems, sum_sems, total_sems) = rest
    place = Place()
    extent = grads.shape[-1]
    core, other = place.core, place.other
    f32, bf16 = jnp.float32, jnp.bfloat16
    across = place.tiles
    greet(place, (place.chip(across),))
    margins = {5: (1, 1), 7: (3, TILE_COLS), 2: (0, 1), 8: (4, TILE_COLS + 1), 6: (2, TILE_COLS)}
    order = ((1, 1), (1, 0), (0, 0), (0, 1))
    needs = {(1, 1): (), (1, 0): (1,), (0, 0): (0, 2, 4), (0, 1): (3,)}
    pair_copies = {}
    for k in [4, *margins, 3, 0, 1]:
        pair_copies[k] = remote(grads.at[other, k], pair.at[k], pair_sems, k, place.sibling())
        pair_copies[k].start()
    edge_copies = {}
    sum_copies = {}

    def send_sum(i, j):
        k = BAND * i + j
        at = 2 * i + j
        pair_copies[k].wait_recv()
        value = grads[core, k].astype(f32) + pair[k].astype(f32)
        for m in needs[i, j]:
            edge_copies[m].wait_recv()
            value = value + edges_in[m].astype(f32)
        sums[at] = value.astype(bf16)
        sum_copies[at] = remote(sums.at[at], sums_in.at[at], sum_sems, at, place.chip(across))
        sum_copies[at].start()

    send_sum(1, 1)
    for k, (m, steps) in margins.items():
        pair_copies[k].wait_recv()
        edges[m] = (grads[core, k].astype(f32) + pair[k].astype(f32)).astype(bf16)
        edge_copies[m] = along(
            place, steps, edges.at[m], edges_in.at[m], edges_via, m,
            edge_sems, edge_via_sems, edge_on_sems,
        )
        edge_copies[m].start()
    hand_on(edge_copies[1])
    send_sum(1, 0)
    for m in (3, 0, 4, 2):
        hand_on(edge_copies[m])
    send_sum(0, 0)
    send_sum(0, 1)

    total_copies = {}
    halo_copies = {}
    for i, j in order:
        at = 2 * i + j
        sum_copies[at].wait_recv()
        total = (sums[at].astype(f32) + sums_in[at].astype(f32)).astype(bf16)
        totals[at] = total
        total_copies[at] = remote(
            totals.at[at], totals_in.at[at], total_sems, at, place.sibling()
        )
        total_copies[at].start()
        fresh = block_of(tile, core, i, j, extent)[...] - LEARNING_RATE * total.astype(f32)
        block_of(refined, core, i, j, extent)[...] = fresh
        if not last and (i, j) != (1, 1):
            outgoing[at] = fresh.astype(bf16)
            send_halos(
                place, halo_copies, i, j, outgoing, halo, halo_via,
                halo_sems, halo_via_sems, halo_on_sems,
            )
            if (i, j) == (0, 0):
                hand_on(halo_copies[RIGHT + 1])
    if not last:
        for piece in HALO_ORDER[1:]:
            hand_on(halo_copies[piece])
    for i, j in order:
        at = 2 * i + j
        total_copies[at].wait_recv()
        block_of(refined, other, i, j, extent)[...] = block_of(tile, other, i, j, extent)[
            ...
        ] - LEARNING_RATE * totals_in[at].astype(f32)
    if not last:
        pass_halos(place, halo, halo_copies, pass_sems)
    for group in (pair_copies, edge_copies, sum_copies, total_copies):
        for copy in group.values():
            copy.wait_send()


def sems(count):
    return pltpu.SemaphoreType.DMA((2, count))


def first_halo(tile, patterns, split):
    extent = patterns.shape[-1]
    vmem = pl.BlockSpec(memory_space=pltpu.VMEM)
    return pl.pallas_call(
        first_halo_kernel,
        out_shape=(
            jax.ShapeDtypeStruct((2, PIECES, extent, extent), jnp.bfloat16),
            jax.ShapeDtypeStruct(patterns.shape, patterns.dtype),
        ),
        in_specs=[vmem] * 3,
        out_specs=(vmem,) * 2,
        scratch_shapes=[
            pltpu.VMEM((4, extent, extent), jnp.bfloat16),
            pltpu.VMEM((PIECES, extent, extent), jnp.bfloat16),
            sems(PIECES),
            sems(PIECES),
            pltpu.SemaphoreType.DMA((PIECES,)),
            sems(PIECES),
        ],
        compiler_params=pltpu.CompilerParams(
            collective_id=0, has_side_effects=True, vmem_limit_bytes=40 * 1024 * 1024
        ),
    )(tile, patterns, split)


def reduce_and_update(grads, tile, last):
    extent = grads.shape[-1]
    vmem = pl.BlockSpec(memory_space=pltpu.VMEM)

    def blocks(count):
        return pltpu.VMEM((count, extent, extent), jnp.bfloat16)

    onward = pltpu.SemaphoreType.DMA((PIECES,))
    shapes = [jax.ShapeDtypeStruct(tile.shape, tile.dtype)]
    scratch = []
    if not last:
        shapes.append(jax.ShapeDtypeStruct((2, PIECES, extent, extent), jnp.bfloat16))
        scratch += [blocks(4), blocks(PIECES), sems(PIECES), sems(PIECES), onward, sems(PIECES)]
    scratch += [blocks(BAND * BAND), blocks(PIECES), blocks(PIECES), blocks(PIECES)]
    scratch += [blocks(4), blocks(4), blocks(4), blocks(4)]
    scratch += [sems(BAND * BAND), sems(PIECES), sems(PIECES), onward, sems(4), sems(4)]
    return pl.pallas_call(
        functools.partial(reduce_kernel, last),
        out_shape=tuple(shapes),
        in_specs=[vmem, vmem],
        out_specs=(vmem,) * len(shapes),
        scratch_shapes=scratch,
        compiler_params=pltpu.CompilerParams(
            collective_id=2 if last else 1,
            has_side_effects=True,
            vmem_limit_bytes=40 * 1024 * 1024,
        ),
    )(grads, tile)


def shards(object_tiles, probe, patterns, corners, counts):
    tile = object_tiles[0]
    extent = probe.shape[1]
    table, split = tables(extent)
    halo, ordered = first_halo(tile, patterns, split)
    for repeat in range(ITERS):
        grads = slot_gradients(tile, halo, probe, ordered, corners, counts, table)
        tile, *rest = reduce_and_update(grads, tile, repeat == ITERS - 1)
        if rest:
            halo = rest[0]
    return tile[None]


def solution(mesh):
    return jax.shard_map(
        shards,
        mesh=mesh,
        in_specs=(
            P("tile", None, None, None),
            P(),
            P(("tile", "pos"), None, None),
            P(("tile", "pos"), None),
            P(("tile", "pos")),
        ),
        out_specs=P("tile", None, None, None),
        check_vma=False,
    )
```

```python
import functools
import math

import jax
import jax.numpy as jnp
import numpy as np
from jax import lax
from jax.experimental import pallas as pl
from jax.experimental.pallas import tpu as pltpu
from jax.sharding import PartitionSpec as P

TILE_COLS = 8
ITERS = 2
LEARNING_RATE = 0.03
LANES = 128
SUBLANES = 8
CHUNK = 32
GROUP = 16
BAND = 3
RIGHT, LOWER, DIAG, PIECES = 0, 2, 4, 5
PLANE = 16
AHEAD = 2
MESH = pl.DeviceIdType.MESH


def tables(extent):
    counter = np.arange(extent, dtype=np.int64)
    phases = counter[:, None] * counter[None, :] % extent
    angles = phases.astype(np.float64) * (2.0 * math.pi / extent)
    factor = 1.0 / math.sqrt(extent)
    cosine = np.cos(angles) * factor
    sine_neg = -np.sin(angles) * factor
    matrices = []
    for parity in range(2):
        c = cosine[:extent // 2, parity::2]
        d = sine_neg[:extent // 2, parity::2]
        matrices.append(np.block([[c, d], [-d, c]]))
    matrices += [matrices[0].T, matrices[1].T]
    rows = np.arange(extent).reshape(2, -1, GROUP).swapaxes(0, 1).reshape(-1)
    matrices += [matrices[at][rows] for at in range(4)]
    order = np.concatenate([counter[0::2], counter[1::2]])
    split = (counter[:, None] == order[None, :]).astype(np.float32)
    return jnp.asarray(np.stack(matrices), jnp.bfloat16), jnp.asarray(
        np.stack([split, split.T]), jnp.bfloat16
    )


def slots_kernel(
    reorder, corners, counts, tile, halo, probe, patterns, table, *rest,
):
    if reorder:
        split, grad_blocks, ordered, *rest = rest
    else:
        grad_blocks, *rest = rest
        ordered = patterns
    image, grad, padded, rolled, wave, half = rest
    extent = probe.shape[1]
    edge = tile.shape[1]
    own = edge // LANES
    margin = extent // LANES
    mid_row = extent // 2
    f32 = jnp.float32
    for ch in range(2):
        for b in range(own):
            cols = slice(b * LANES, (b + 1) * LANES)
            image[b, ch, :edge] = tile[ch, :, cols]
            inner = slice(b % margin * LANES, (b % margin + 1) * LANES)
            image[b, ch, edge:] = halo[ch, LOWER + b // margin, :, inner].astype(f32)
        for b in range(margin):
            cols = slice(b * LANES, (b + 1) * LANES)
            for i in range(edge // extent):
                image[own + b, ch, i * extent:(i + 1) * extent] = halo[ch, RIGHT + i, :, cols].astype(f32)
            image[own + b, ch, edge:] = halo[ch, DIAG, :, cols].astype(f32)
            padded[ch, b, :SUBLANES] = probe[ch, extent - SUBLANES:, cols]
            padded[ch, b, SUBLANES:] = probe[ch, :, cols]
    grad[...] = jnp.zeros_like(grad)

    class Slot:
        def __init__(self, g, lane):
            self.g, self.lane = g, lane
            row, col = corners[g, 0], corners[g, 1]
            self.row_off = lax.rem(row, SUBLANES)
            self.col_off = lax.rem(col, LANES)
            self.row_at = pl.multiple_of(row - self.row_off, SUBLANES)
            self.block = lax.div(col, LANES)
            self.keep = lax.broadcasted_iota(jnp.int32, (CHUNK, LANES), 1) >= self.col_off
            self.keep8 = lax.broadcasted_iota(jnp.int32, (SUBLANES, LANES), 1) >= self.col_off
            self.stay8 = lax.broadcasted_iota(jnp.int32, (SUBLANES, LANES), 0) >= self.row_off
            self.below = pl.ds(pl.multiple_of(self.row_at + extent, SUBLANES), SUBLANES)

        def rows(self, i, number=CHUNK):
            return pl.ds(pl.multiple_of(self.row_at + i, SUBLANES), number)

        def illuminate(self):
            keep, keep8, stay8, block, lane = self.keep, self.keep8, self.stay8, self.block, self.lane
            for i in range(0, extent, CHUNK):
                here = slice(i, i + CHUNK)
                shifted = []
                for ch in range(2):
                    turned = [
                        pltpu.roll(
                            padded[ch, b, pl.ds(SUBLANES - self.row_off + i, CHUNK), :],
                            self.col_off, 1,
                        )
                        for b in range(2)
                    ]
                    shifted.append((
                        jnp.where(keep, turned[0], turned[1]), jnp.where(keep, turned[1], turned[0])
                    ))
                    rolled[lane, ch, 0, here] = shifted[ch][0]
                    rolled[lane, ch, 1, here] = shifted[ch][1]
                rows = self.rows(i)
                crops = []
                for ch in range(2):
                    left = jnp.where(
                        keep, image[block, ch, rows, :], image[block + 2, ch, rows, :]
                    )
                    mid = image[block + 1, ch, rows, :]
                    if i == 0:
                        below = self.below
                        left8 = jnp.where(
                            keep8, image[block, ch, below, :], image[block + 2, ch, below, :]
                        )
                        mid8 = image[block + 1, ch, below, :]
                        left = jnp.concatenate(
                            [jnp.where(stay8, left[:SUBLANES], left8), left[SUBLANES:]], 0
                        )
                        mid = jnp.concatenate(
                            [jnp.where(stay8, mid[:SUBLANES], mid8), mid[SUBLANES:]], 0
                        )
                    crops.append((left, mid))
                real = [
                    shifted[0][b] * crops[0][b] - shifted[1][b] * crops[1][b] for b in range(2)
                ]
                imag = [
                    shifted[0][b] * crops[1][b] + shifted[1][b] * crops[0][b] for b in range(2)
                ]
                wave[lane, 0, here, :LANES] = (real[0] + real[1]).astype(jnp.bfloat16)
                wave[lane, 0, here, LANES:] = (imag[0] + imag[1]).astype(jnp.bfloat16)
                wave[lane, 1, here, :LANES] = (real[0] - real[1]).astype(jnp.bfloat16)
                wave[lane, 1, here, LANES:] = (imag[0] - imag[1]).astype(jnp.bfloat16)

        def along_rows(self):
            lane = self.lane
            for q in range(2):
                freq = jnp.dot(wave[lane, q], table[q], preferred_element_type=f32)
                near, far = freq[:mid_row], freq[mid_row:]
                cols = slice(q * LANES, (q + 1) * LANES)
                for r, value in enumerate((near + far, near - far)):
                    half[lane, r, :mid_row, cols] = value[:, :LANES].astype(jnp.bfloat16)
                    half[lane, r, mid_row:, cols] = value[:, LANES:].astype(jnp.bfloat16)

        def along_columns(self, at, r):
            return jnp.dot(table[at + r], half[self.lane, r], preferred_element_type=f32)

        def push(self):
            lane = self.lane
            for r in range(2):
                freq = self.along_columns(6, r)
                for i in range(0, mid_row, GROUP):
                    here = slice(r * mid_row + i, r * mid_row + i + GROUP)
                    real = freq[2 * i:2 * i + GROUP]
                    imag = freq[2 * i + GROUP:2 * i + 2 * GROUP]
                    misfit = real * real + imag * imag - ordered[self.g, here].astype(f32)
                    real = (real * misfit).astype(jnp.bfloat16)
                    imag = (imag * misfit).astype(jnp.bfloat16)
                    for q in range(2):
                        cols = slice(q * LANES, (q + 1) * LANES)
                        wave[lane, q, here, :LANES] = real[:, cols]
                        wave[lane, q, here, LANES:] = imag[:, cols]

        def back_along_rows(self):
            lane = self.lane
            even = jnp.dot(wave[lane, 0], table[2], preferred_element_type=f32)
            odd = jnp.dot(wave[lane, 1], table[3], preferred_element_type=f32)
            for b, value in enumerate((even + odd, even - odd)):
                cols = slice(b * LANES, (b + 1) * LANES)
                for r in range(2):
                    rows = slice(r * mid_row, (r + 1) * mid_row)
                    half[lane, r, :mid_row, cols] = value[rows, :LANES].astype(jnp.bfloat16)
                    half[lane, r, mid_row:, cols] = value[rows, LANES:].astype(jnp.bfloat16)

        def gather(self):
            keep, keep8, stay8 = self.keep[:GROUP], self.keep8, self.stay8
            block, lane = self.block, self.lane
            even, odd = self.along_columns(4, 0), self.along_columns(4, 1)
            for i in range(0, extent, GROUP):
                here = slice(i, i + GROUP)
                rows = self.rows(i, GROUP)
                both = jnp.add if i < mid_row else jnp.subtract
                at = 2 * (i % mid_row)
                for b in range(2):
                    cols = slice(b * LANES, (b + 1) * LANES)
                    real = both(even[at:at + GROUP, cols], odd[at:at + GROUP, cols])
                    at_imag = slice(at + GROUP, at + 2 * GROUP)
                    imag = both(even[at_imag, cols], odd[at_imag, cols])
                    p_real = rolled[lane, 0, b, here]
                    p_imag = rolled[lane, 1, b, here]
                    parts = (p_real * real + p_imag * imag, p_real * imag - p_imag * real)
                    for ch in range(2):
                        value = parts[ch]
                        if i == 0:
                            spill = jnp.where(stay8, 0.0, value[:SUBLANES])
                            value = jnp.concatenate(
                                [jnp.where(stay8, value[:SUBLANES], 0.0), value[SUBLANES:]], 0
                            )
                            below = self.below
                            if b == 0:
                                grad[block, ch, below, :] += jnp.where(keep8, spill, 0.0)
                                grad[block + 2, ch, below, :] += jnp.where(keep8, 0.0, spill)
                            else:
                                grad[block + 1, ch, below, :] += spill
                        if b == 0:
                            grad[block, ch, rows, :] += jnp.where(keep, value, 0.0)
                            grad[block + 2, ch, rows, :] += jnp.where(keep, 0.0, value)
                        else:
                            grad[block + 1, ch, rows, :] += value

        def order(self):
            by_columns = jnp.dot(patterns[self.g], split[0], preferred_element_type=f32)
            by_rows = jnp.dot(
                split[1], by_columns.astype(jnp.bfloat16), preferred_element_type=f32
            )
            ordered[self.g] = by_rows.astype(jnp.bfloat16)

        def stages(self):
            return ((self.order,) if reorder else ()) + self.steps()

        def steps(self):
            return (
                self.illuminate,
                self.along_rows,
                self.push,
                self.back_along_rows,
                self.gather,
            )

    def pair(p, carry):
        ahead, behind = Slot(2 * p, 0).stages(), Slot(2 * p + 1, 1).stages()
        for a, b in zip(ahead, behind):
            a()
            b()
        return carry

    live = counts[0]
    lax.fori_loop(0, lax.div(live, 2), pair, 0)

    @pl.when(lax.rem(live, 2) == 1)
    def _():
        for stage in Slot(live - 1, 0).stages():
            stage()

    for ch in range(2):
        for i in range(BAND):
            rows = slice(i * extent, (i + 1) * extent)
            for b in range(BAND * margin):
                cols = slice(b % margin * LANES, (b % margin + 1) * LANES)
                grad_blocks[ch, i * BAND + b // margin, :, cols] = grad[b, ch, rows].astype(
                    jnp.bfloat16
                )


def slot_gradients(tile, halo, probe, patterns, corners, counts, table, split=None):
    extent = probe.shape[1]
    edge = tile.shape[1]
    total = edge + extent
    blocks = total // LANES
    f32, bf16 = jnp.float32, jnp.bfloat16
    vmem = pl.BlockSpec(memory_space=pltpu.VMEM)
    smem = pl.BlockSpec(memory_space=pltpu.SMEM)
    reorder = split is not None
    shapes = [jax.ShapeDtypeStruct((2, BAND * BAND, extent, extent), bf16)]
    operands = [corners, counts, tile, halo, probe, patterns, table]
    if reorder:
        shapes.append(jax.ShapeDtypeStruct(patterns.shape, patterns.dtype))
        operands.append(split)
    return pl.pallas_call(
        functools.partial(slots_kernel, reorder),
        out_shape=tuple(shapes),
        in_specs=[smem, smem] + [vmem] * (len(operands) - 2),
        out_specs=(vmem,) * len(shapes),
        scratch_shapes=[
            pltpu.VMEM((blocks, 2, total, LANES), f32),
            pltpu.VMEM((blocks, 2, total, LANES), f32),
            pltpu.VMEM((2, 2, extent + SUBLANES, LANES), f32),
            pltpu.VMEM((2, 2, 2, extent, LANES), f32),
            pltpu.VMEM((2, 2, extent, extent), bf16),
            pltpu.VMEM((2, 2, extent, extent), bf16),
        ],
        compiler_params=pltpu.CompilerParams(vmem_limit_bytes=40 * 1024 * 1024),
        cost_estimate=pl.CostEstimate(
            flops=4 * 4 * 2 * extent**3 * 2, bytes_accessed=8 * 2**20, transcendentals=0
        ),
    )(*operands)


class Place:
    def __init__(self):
        self.tiles = lax.axis_size("tile")
        self.chips = self.tiles * (lax.axis_size("pos") // 2)
        pos = lax.axis_index("pos")
        self.core = lax.rem(pos, 2)
        self.other = 1 - self.core
        self.flat = lax.div(pos, 2) * self.tiles + lax.axis_index("tile")
        self.local = lax.rem(self.flat, PLANE)
        self.column = lax.rem(self.flat + TILE_COLS + TILE_COLS // 2, TILE_COLS)

    def at(self, flat, core):
        return lax.rem(flat, self.tiles), lax.div(flat, self.tiles) * 2 + core

    def device(self, steps, core):
        return self.at(lax.rem(self.flat + steps + self.chips, self.chips), core)

    def sibling(self):
        return self.device(0, self.other)

    def chip(self, steps):
        return self.device(steps, self.core)

    def in_plane(self, steps):
        local = lax.rem(self.local + steps + PLANE, PLANE)
        return self.at(self.flat - self.local + local, self.core)

    def relayed(self, steps):
        return abs(steps) == 1 or steps == -TILE_COLS

    def legs(self, steps):
        return self.in_plane(steps), self.chip(PLANE if steps > 0 else -PLANE)

    def starts(self, steps, local):
        if steps == 1:
            return local == PLANE - 1
        return jnp.logical_and(local == 0, self.core == 1)

    def leaves(self, steps):
        return self.starts(steps, self.local)

    def hands_on(self, steps):
        return self.starts(steps, lax.rem(self.local - steps + PLANE, PLANE))

    def has_source(self, steps):
        return self.column != (0 if steps > 0 else TILE_COLS - 1)

    def has_target(self, steps):
        return self.column != (TILE_COLS - 1 if steps > 0 else 0)


def greet(place, extra=()):
    devices = [place.sibling(), place.chip(PLANE), place.chip(-PLANE), *extra]
    for sign in (1, -1):
        devices += [place.in_plane(sign), place.in_plane(sign * TILE_COLS)]
        devices += [place.chip(sign * steps) for steps in (1, TILE_COLS, TILE_COLS + 1)]
    barrier = pltpu.get_barrier_semaphore()
    for device in devices:
        pl.semaphore_signal(barrier, inc=1, device_id=device, device_id_type=MESH)
    pl.semaphore_wait(barrier, len(devices))


def halo_targets(i, j):
    targets = []
    if j == 0:
        targets.append((RIGHT + i, -1))
    if i == 0:
        targets.append((LOWER + j, -TILE_COLS))
    if i == 0 and j == 0:
        targets.append((DIAG, -TILE_COLS - 1))
    return targets


def remote(source, target, sems, at, device):
    return pltpu.make_async_remote_copy(
        src_ref=source,
        dst_ref=target,
        send_sem=sems.at[0, at],
        recv_sem=sems.at[1, at],
        device_id=device,
        device_id_type=MESH,
    )


class Routed:
    def __init__(self, place, steps, source, target, via, at, direct_sems, via_sems, on_sems):
        self.target = target
        self.direct = remote(source, target, direct_sems, at, place.chip(steps))
        self.sends = self.receives = True
        if abs(steps) == 1 or abs(steps) == TILE_COLS + 1:
            self.sends, self.receives = place.has_target(steps), place.has_source(steps)
        self.relayed = place.relayed(steps)
        if self.relayed:
            first, second = place.legs(steps)
            self.away = remote(source, via.at[at], via_sems, at, first)
            self.onward = pltpu.make_async_remote_copy(
                src_ref=via.at[at],
                dst_ref=target,
                send_sem=on_sems.at[at],
                recv_sem=direct_sems.at[1, at],
                device_id=second,
                device_id_type=MESH,
            )
            leaves = place.leaves(steps)
            self.leaves = jnp.logical_and(self.sends, leaves)
            self.stays = jnp.logical_and(self.sends, jnp.logical_not(leaves))
            self.hands_on = place.hands_on(steps)
        else:
            self.stays = self.sends

    def start(self):
        if self.relayed:
            pl.when(self.leaves)(self.away.start)
        pl.when(self.stays)(self.direct.start)

    def hand_on(self):
        if self.relayed:

            @pl.when(self.hands_on)
            def _():
                self.away.wait_recv()
                self.onward.start()

    def wait_recv(self):
        pl.when(self.receives)(self.direct.wait_recv)
        if self.receives is not True:

            @pl.when(jnp.logical_not(self.receives))
            def _():
                self.target[...] = jnp.zeros(self.target.shape, self.target.dtype)

    def wait_send(self):
        if self.relayed:
            pl.when(self.leaves)(self.away.wait_send)
            pl.when(self.hands_on)(self.onward.wait_send)
        pl.when(self.stays)(self.direct.wait_send)


def block_of(ref, channel, i, j, extent):
    return ref.at[channel, i * extent:(i + 1) * extent, j * extent:(j + 1) * extent]


HALO_ORDER = (RIGHT + 1, RIGHT, LOWER, DIAG, LOWER + 1)


def send_halos(place, copies, i, j, outgoing, halo, via, halo_sems, via_sems, on_sems):
    for piece, steps in halo_targets(i, j):
        copies[piece] = Routed(
            place, steps, outgoing.at[2 * i + j], halo.at[place.core, piece], via, piece,
            halo_sems, via_sems, on_sems,
        )
        copies[piece].start()


def pass_halos(place, halo, copies, pass_sems):
    passes = []
    for piece in HALO_ORDER:
        copies[piece].wait_recv()
        mine = halo.at[place.core, piece]
        passes.append(remote(mine, mine, pass_sems, piece, place.sibling()))
        passes[-1].start()
    for copy in passes:
        copy.wait()
    for copy in copies.values():
        copy.wait_send()


def first_halo_kernel(
    tile, halo, outgoing, via, halo_sems, via_sems, on_sems, pass_sems,
):
    place = Place()
    extent = outgoing.shape[-1]
    greet(place)
    copies = {}
    for i, j in ((0, 0), (1, 0), (0, 1)):
        outgoing[2 * i + j] = block_of(tile, place.core, i, j, extent)[...].astype(jnp.bfloat16)
        send_halos(place, copies, i, j, outgoing, halo, via, halo_sems, via_sems, on_sems)
    for piece in (RIGHT, RIGHT + 1, LOWER, LOWER + 1):
        copies[piece].hand_on()
    pass_halos(place, halo, copies, pass_sems)


def reduce_kernel(last, grads, tile, refined, *rest):
    if not last:
        halo, outgoing, halo_via, halo_sems, halo_via_sems, halo_on_sems, pass_sems = rest[:7]
        rest = rest[7:]
    (pair, edges, edges_in, edges_via, sums, sums_in, totals, totals_in,
     pair_sems, edge_sems, edge_via_sems, edge_on_sems,
     sum_sems, total_sems) = rest
    place = Place()
    extent = grads.shape[-1]
    core, other = place.core, place.other
    f32, bf16 = jnp.float32, jnp.bfloat16
    across = place.tiles
    greet(place, (place.chip(across),))
    margins = {5: (1, 1), 7: (3, TILE_COLS), 2: (0, 1), 8: (4, TILE_COLS + 1), 6: (2, TILE_COLS)}
    order = ((1, 1), (1, 0), (0, 0), (0, 1))
    needs = {(1, 1): (), (1, 0): (1,), (0, 0): (0, 2, 4), (0, 1): (3,)}
    pair_copies = {}
    for k in [4, *margins, 3, 0, 1]:
        pair_copies[k] = remote(grads.at[other, k], pair.at[k], pair_sems, k, place.sibling())
        pair_copies[k].start()
    edge_copies = {}
    sum_copies = {}
    under_way = []

    def send_sum(i, j):
        k = BAND * i + j
        at = 2 * i + j
        pair_copies[k].wait_recv()
        value = grads[core, k].astype(f32) + pair[k].astype(f32)
        for m in needs[i, j]:
            edge_copies[m].wait_recv()
            value = value + edges_in[m].astype(f32)
        sums[at] = value.astype(bf16)
        sum_copies[at] = remote(sums.at[at], sums_in.at[at], sum_sems, at, place.chip(across))
        if len(under_way) >= AHEAD:
            under_way.pop(0).wait_send()
        sum_copies[at].start()
        under_way.append(sum_copies[at])

    send_sum(1, 1)
    for k, (m, steps) in margins.items():
        pair_copies[k].wait_recv()
        edges[m] = (grads[core, k].astype(f32) + pair[k].astype(f32)).astype(bf16)
        edge_copies[m] = Routed(
            place, steps, edges.at[m], edges_in.at[m], edges_via, m,
            edge_sems, edge_via_sems, edge_on_sems,
        )
        edge_copies[m].start()
    edge_copies[1].hand_on()
    send_sum(1, 0)
    edge_copies[0].hand_on()
    for i, j in order[2:]:
        send_sum(i, j)

    total_copies = {}
    halo_copies = {}
    for i, j in order:
        at = 2 * i + j
        sum_copies[at].wait_recv()
        total = (sums[at].astype(f32) + sums_in[at].astype(f32)).astype(bf16)
        totals[at] = total
        total_copies[at] = remote(
            totals.at[at], totals_in.at[at], total_sems, at, place.sibling()
        )
        total_copies[at].start()
        fresh = block_of(tile, core, i, j, extent)[...] - LEARNING_RATE * total.astype(f32)
        block_of(refined, core, i, j, extent)[...] = fresh
        if not last and (i, j) != (1, 1):
            outgoing[at] = fresh.astype(bf16)
            send_halos(
                place, halo_copies, i, j, outgoing, halo, halo_via,
                halo_sems, halo_via_sems, halo_on_sems,
            )
            if (i, j) == (0, 0):
                for piece in (RIGHT + 1, LOWER, RIGHT):
                    halo_copies[piece].hand_on()
    if not last:
        halo_copies[LOWER + 1].hand_on()
    for i, j in order:
        at = 2 * i + j
        total_copies[at].wait_recv()
        block_of(refined, other, i, j, extent)[...] = block_of(tile, other, i, j, extent)[
            ...
        ] - LEARNING_RATE * totals_in[at].astype(f32)
    if not last:
        pass_halos(place, halo, halo_copies, pass_sems)
    for copy in (*pair_copies.values(), *edge_copies.values(), *under_way, *total_copies.values()):
        copy.wait_send()


def sems(count):
    return pltpu.SemaphoreType.DMA((2, count))


def first_halo(tile, extent):
    vmem = pl.BlockSpec(memory_space=pltpu.VMEM)
    return pl.pallas_call(
        first_halo_kernel,
        out_shape=jax.ShapeDtypeStruct((2, PIECES, extent, extent), jnp.bfloat16),
        in_specs=[vmem],
        out_specs=vmem,
        scratch_shapes=[
            pltpu.VMEM((4, extent, extent), jnp.bfloat16),
            pltpu.VMEM((PIECES, extent, extent), jnp.bfloat16),
            sems(PIECES),
            sems(PIECES),
            pltpu.SemaphoreType.DMA((PIECES,)),
            sems(PIECES),
        ],
        compiler_params=pltpu.CompilerParams(
            collective_id=0, has_side_effects=True, vmem_limit_bytes=40 * 1024 * 1024
        ),
    )(tile)


def reduce_and_update(grads, tile, last):
    extent = grads.shape[-1]
    vmem = pl.BlockSpec(memory_space=pltpu.VMEM)

    def blocks(count):
        return pltpu.VMEM((count, extent, extent), jnp.bfloat16)

    onward = pltpu.SemaphoreType.DMA((PIECES,))
    shapes = [jax.ShapeDtypeStruct(tile.shape, tile.dtype)]
    scratch = []
    if not last:
        shapes.append(jax.ShapeDtypeStruct((2, PIECES, extent, extent), jnp.bfloat16))
        scratch += [blocks(4), blocks(PIECES), sems(PIECES), sems(PIECES), onward, sems(PIECES)]
    scratch += [blocks(BAND * BAND), blocks(PIECES), blocks(PIECES), blocks(PIECES)]
    scratch += [blocks(4)] * 4
    scratch += [sems(BAND * BAND), sems(PIECES), sems(PIECES), onward]
    scratch += [sems(4), sems(4)]
    return pl.pallas_call(
        functools.partial(reduce_kernel, last),
        out_shape=tuple(shapes),
        in_specs=[vmem, vmem],
        out_specs=(vmem,) * len(shapes),
        scratch_shapes=scratch,
        compiler_params=pltpu.CompilerParams(
            collective_id=2 if last else 1,
            has_side_effects=True,
            vmem_limit_bytes=40 * 1024 * 1024,
        ),
    )(grads, tile)


def shards(object_tiles, probe, patterns, corners, counts):
    tile = object_tiles[0]
    extent = probe.shape[1]
    table, split = tables(extent)
    halo = first_halo(tile, extent)
    for repeat in range(ITERS):
        grads, *ordered = slot_gradients(
            tile, halo, probe, patterns, corners, counts, table, None if repeat else split
        )
        if ordered:
            patterns = ordered[0]
        tile, *rest = reduce_and_update(grads, tile, repeat == ITERS - 1)
        if rest:
            halo = rest[0]
    return tile[None]


def solution(mesh):
    return jax.shard_map(
        shards,
        mesh=mesh,
        in_specs=(
            P("tile", None, None, None),
            P(),
            P(("tile", "pos"), None, None),
            P(("tile", "pos"), None),
            P(("tile", "pos")),
        ),
        out_specs=P("tile", None, None, None),
        check_vma=False,
    )
```

```python
import functools
import math

import jax
import jax.numpy as jnp
import numpy as np
from jax import lax
from jax.experimental import pallas as pl
from jax.experimental.pallas import tpu as pltpu
from jax.sharding import PartitionSpec as P

TILE_COLS = 8
ITERS = 2
LEARNING_RATE = 0.03
LANES = 128
SUBLANES = 8
CHUNK = 32
GROUP = 16
BAND = 3
RIGHT, LOWER, DIAG, PIECES = 0, 2, 4, 5
PLANE = 16
AHEAD = 2
MESH = pl.DeviceIdType.MESH


def tables(extent):
    counter = np.arange(extent, dtype=np.int64)
    phases = counter[:, None] * counter[None, :] % extent
    angles = phases.astype(np.float64) * (2.0 * math.pi / extent)
    factor = 1.0 / math.sqrt(extent)
    cosine = np.cos(angles) * factor
    sine_neg = -np.sin(angles) * factor
    matrices = []
    for parity in range(2):
        c = cosine[:extent // 2, parity::2]
        d = sine_neg[:extent // 2, parity::2]
        matrices.append(np.block([[c, d], [-d, c]]))
    matrices += [matrices[0].T, matrices[1].T]
    rows = np.arange(extent).reshape(2, -1, GROUP).swapaxes(0, 1).reshape(-1)
    matrices += [matrices[at][rows] for at in range(4)]
    order = np.concatenate([counter[0::2], counter[1::2]])
    split = (counter[:, None] == order[None, :]).astype(np.float32)
    return jnp.asarray(np.stack(matrices), jnp.bfloat16), jnp.asarray(
        np.stack([split, split.T]), jnp.bfloat16
    )


def slots_kernel(
    reorder, corners, counts, tile, halo, probe, patterns, table, *rest,
):
    if reorder:
        split, grad_blocks, ordered, *rest = rest
    else:
        grad_blocks, *rest = rest
        ordered = patterns
    image, grad, padded, rolled, wave, half = rest
    extent = probe.shape[1]
    edge = tile.shape[1]
    own = edge // LANES
    margin = extent // LANES
    mid_row = extent // 2
    f32 = jnp.float32
    for ch in range(2):
        for b in range(own):
            cols = slice(b * LANES, (b + 1) * LANES)
            image[b, ch, :edge] = tile[ch, :, cols]
            inner = slice(b % margin * LANES, (b % margin + 1) * LANES)
            image[b, ch, edge:] = halo[ch, LOWER + b // margin, :, inner].astype(f32)
        for b in range(margin):
            cols = slice(b * LANES, (b + 1) * LANES)
            for i in range(edge // extent):
                image[own + b, ch, i * extent:(i + 1) * extent] = halo[ch, RIGHT + i, :, cols].astype(f32)
            image[own + b, ch, edge:] = halo[ch, DIAG, :, cols].astype(f32)
            padded[ch, b, :SUBLANES] = probe[ch, extent - SUBLANES:, cols]
            padded[ch, b, SUBLANES:] = probe[ch, :, cols]
    grad[...] = jnp.zeros_like(grad)

    class Slot:
        def __init__(self, g, lane):
            self.g, self.lane = g, lane
            row, col = corners[g, 0], corners[g, 1]
            self.row_off = lax.rem(row, SUBLANES)
            self.col_off = lax.rem(col, LANES)
            self.row_at = pl.multiple_of(row - self.row_off, SUBLANES)
            self.block = lax.div(col, LANES)
            self.keep = lax.broadcasted_iota(jnp.int32, (CHUNK, LANES), 1) >= self.col_off
            self.keep8 = lax.broadcasted_iota(jnp.int32, (SUBLANES, LANES), 1) >= self.col_off
            self.stay8 = lax.broadcasted_iota(jnp.int32, (SUBLANES, LANES), 0) >= self.row_off
            self.below = pl.ds(pl.multiple_of(self.row_at + extent, SUBLANES), SUBLANES)

        def rows(self, i, number=CHUNK):
            return pl.ds(pl.multiple_of(self.row_at + i, SUBLANES), number)

        def illuminate(self):
            keep, keep8, stay8, block, lane = self.keep, self.keep8, self.stay8, self.block, self.lane
            for i in range(0, extent, CHUNK):
                here = slice(i, i + CHUNK)
                shifted = []
                for ch in range(2):
                    turned = [
                        pltpu.roll(
                            padded[ch, b, pl.ds(SUBLANES - self.row_off + i, CHUNK), :],
                            self.col_off, 1,
                        )
                        for b in range(2)
                    ]
                    shifted.append((
                        jnp.where(keep, turned[0], turned[1]), jnp.where(keep, turned[1], turned[0])
                    ))
                    rolled[lane, ch, 0, here] = shifted[ch][0]
                    rolled[lane, ch, 1, here] = shifted[ch][1]
                rows = self.rows(i)
                crops = []
                for ch in range(2):
                    left = jnp.where(
                        keep, image[block, ch, rows, :], image[block + 2, ch, rows, :]
                    )
                    mid = image[block + 1, ch, rows, :]
                    if i == 0:
                        below = self.below
                        left8 = jnp.where(
                            keep8, image[block, ch, below, :], image[block + 2, ch, below, :]
                        )
                        mid8 = image[block + 1, ch, below, :]
                        left = jnp.concatenate(
                            [jnp.where(stay8, left[:SUBLANES], left8), left[SUBLANES:]], 0
                        )
                        mid = jnp.concatenate(
                            [jnp.where(stay8, mid[:SUBLANES], mid8), mid[SUBLANES:]], 0
                        )
                    crops.append((left, mid))
                real = [
                    shifted[0][b] * crops[0][b] - shifted[1][b] * crops[1][b] for b in range(2)
                ]
                imag = [
                    shifted[0][b] * crops[1][b] + shifted[1][b] * crops[0][b] for b in range(2)
                ]
                wave[lane, 0, here, :LANES] = (real[0] + real[1]).astype(jnp.bfloat16)
                wave[lane, 0, here, LANES:] = (imag[0] + imag[1]).astype(jnp.bfloat16)
                wave[lane, 1, here, :LANES] = (real[0] - real[1]).astype(jnp.bfloat16)
                wave[lane, 1, here, LANES:] = (imag[0] - imag[1]).astype(jnp.bfloat16)

        def along_rows(self):
            lane = self.lane
            for q in range(2):
                freq = jnp.dot(wave[lane, q], table[q], preferred_element_type=f32)
                near, far = freq[:mid_row], freq[mid_row:]
                cols = slice(q * LANES, (q + 1) * LANES)
                for r, value in enumerate((near + far, near - far)):
                    half[lane, r, :mid_row, cols] = value[:, :LANES].astype(jnp.bfloat16)
                    half[lane, r, mid_row:, cols] = value[:, LANES:].astype(jnp.bfloat16)

        def along_columns(self, at, r):
            return jnp.dot(table[at + r], half[self.lane, r], preferred_element_type=f32)

        def push(self):
            lane = self.lane
            for r in range(2):
                freq = self.along_columns(6, r)
                for i in range(0, mid_row, GROUP):
                    here = slice(r * mid_row + i, r * mid_row + i + GROUP)
                    real = freq[2 * i:2 * i + GROUP]
                    imag = freq[2 * i + GROUP:2 * i + 2 * GROUP]
                    misfit = real * real + imag * imag - ordered[self.g, here].astype(f32)
                    real = (real * misfit).astype(jnp.bfloat16)
                    imag = (imag * misfit).astype(jnp.bfloat16)
                    for q in range(2):
                        cols = slice(q * LANES, (q + 1) * LANES)
                        wave[lane, q, here, :LANES] = real[:, cols]
                        wave[lane, q, here, LANES:] = imag[:, cols]

        def back_along_rows(self):
            lane = self.lane
            even = jnp.dot(wave[lane, 0], table[2], preferred_element_type=f32)
            odd = jnp.dot(wave[lane, 1], table[3], preferred_element_type=f32)
            for b, value in enumerate((even + odd, even - odd)):
                cols = slice(b * LANES, (b + 1) * LANES)
                for r in range(2):
                    rows = slice(r * mid_row, (r + 1) * mid_row)
                    half[lane, r, :mid_row, cols] = value[rows, :LANES].astype(jnp.bfloat16)
                    half[lane, r, mid_row:, cols] = value[rows, LANES:].astype(jnp.bfloat16)

        def gather(self):
            keep, keep8, stay8 = self.keep[:GROUP], self.keep8, self.stay8
            block, lane = self.block, self.lane
            even, odd = self.along_columns(4, 0), self.along_columns(4, 1)
            for i in range(0, extent, GROUP):
                here = slice(i, i + GROUP)
                rows = self.rows(i, GROUP)
                both = jnp.add if i < mid_row else jnp.subtract
                at = 2 * (i % mid_row)
                for b in range(2):
                    cols = slice(b * LANES, (b + 1) * LANES)
                    real = both(even[at:at + GROUP, cols], odd[at:at + GROUP, cols])
                    at_imag = slice(at + GROUP, at + 2 * GROUP)
                    imag = both(even[at_imag, cols], odd[at_imag, cols])
                    p_real = rolled[lane, 0, b, here]
                    p_imag = rolled[lane, 1, b, here]
                    parts = (p_real * real + p_imag * imag, p_real * imag - p_imag * real)
                    for ch in range(2):
                        value = parts[ch]
                        if i == 0:
                            spill = jnp.where(stay8, 0.0, value[:SUBLANES])
                            value = jnp.concatenate(
                                [jnp.where(stay8, value[:SUBLANES], 0.0), value[SUBLANES:]], 0
                            )
                            below = self.below
                            if b == 0:
                                grad[block, ch, below, :] += jnp.where(keep8, spill, 0.0)
                                grad[block + 2, ch, below, :] += jnp.where(keep8, 0.0, spill)
                            else:
                                grad[block + 1, ch, below, :] += spill
                        if b == 0:
                            grad[block, ch, rows, :] += jnp.where(keep, value, 0.0)
                            grad[block + 2, ch, rows, :] += jnp.where(keep, 0.0, value)
                        else:
                            grad[block + 1, ch, rows, :] += value

        def order(self):
            by_columns = jnp.dot(patterns[self.g], split[0], preferred_element_type=f32)
            by_rows = jnp.dot(
                split[1], by_columns.astype(jnp.bfloat16), preferred_element_type=f32
            )
            ordered[self.g] = by_rows.astype(jnp.bfloat16)

        def stages(self):
            return ((self.order,) if reorder else ()) + self.steps()

        def steps(self):
            return (
                self.illuminate,
                self.along_rows,
                self.push,
                self.back_along_rows,
                self.gather,
            )

    def pair(p, carry):
        ahead, behind = Slot(2 * p, 0).stages(), Slot(2 * p + 1, 1).stages()
        for a, b in zip(ahead, behind):
            a()
            b()
        return carry

    live = counts[0]
    lax.fori_loop(0, lax.div(live, 2), pair, 0)

    @pl.when(lax.rem(live, 2) == 1)
    def _():
        for stage in Slot(live - 1, 0).stages():
            stage()

    for ch in range(2):
        for i in range(BAND):
            rows = slice(i * extent, (i + 1) * extent)
            for b in range(BAND * margin):
                cols = slice(b % margin * LANES, (b % margin + 1) * LANES)
                grad_blocks[ch, i * BAND + b // margin, :, cols] = grad[b, ch, rows].astype(
                    jnp.bfloat16
                )


def slot_gradients(tile, halo, probe, patterns, corners, counts, table, split=None):
    extent = probe.shape[1]
    edge = tile.shape[1]
    total = edge + extent
    blocks = total // LANES
    f32, bf16 = jnp.float32, jnp.bfloat16
    vmem = pl.BlockSpec(memory_space=pltpu.VMEM)
    smem = pl.BlockSpec(memory_space=pltpu.SMEM)
    reorder = split is not None
    shapes = [jax.ShapeDtypeStruct((2, BAND * BAND, extent, extent), bf16)]
    operands = [corners, counts, tile, halo, probe, patterns, table]
    if reorder:
        shapes.append(jax.ShapeDtypeStruct(patterns.shape, patterns.dtype))
        operands.append(split)
    return pl.pallas_call(
        functools.partial(slots_kernel, reorder),
        out_shape=tuple(shapes),
        in_specs=[smem, smem] + [vmem] * (len(operands) - 2),
        out_specs=(vmem,) * len(shapes),
        scratch_shapes=[
            pltpu.VMEM((blocks, 2, total, LANES), f32),
            pltpu.VMEM((blocks, 2, total, LANES), f32),
            pltpu.VMEM((2, 2, extent + SUBLANES, LANES), f32),
            pltpu.VMEM((2, 2, 2, extent, LANES), f32),
            pltpu.VMEM((2, 2, extent, extent), bf16),
            pltpu.VMEM((2, 2, extent, extent), bf16),
        ],
        compiler_params=pltpu.CompilerParams(vmem_limit_bytes=40 * 1024 * 1024),
        cost_estimate=pl.CostEstimate(
            flops=4 * 4 * 2 * extent**3 * 2, bytes_accessed=8 * 2**20, transcendentals=0
        ),
    )(*operands)


class Place:
    def __init__(self):
        self.tiles = lax.axis_size("tile")
        self.chips = self.tiles * (lax.axis_size("pos") // 2)
        pos = lax.axis_index("pos")
        self.core = lax.rem(pos, 2)
        self.other = 1 - self.core
        self.flat = lax.div(pos, 2) * self.tiles + lax.axis_index("tile")
        self.local = lax.rem(self.flat, PLANE)
        self.column = lax.rem(self.flat + TILE_COLS + TILE_COLS // 2, TILE_COLS)

    def at(self, flat, core):
        return lax.rem(flat, self.tiles), lax.div(flat, self.tiles) * 2 + core

    def device(self, steps, core):
        return self.at(lax.rem(self.flat + steps + self.chips, self.chips), core)

    def sibling(self):
        return self.device(0, self.other)

    def chip(self, steps):
        return self.device(steps, self.core)

    def in_plane(self, steps):
        local = lax.rem(self.local + steps + PLANE, PLANE)
        return self.at(self.flat - self.local + local, self.core)

    def relayed(self, steps):
        return abs(steps) == 1

    def legs(self, steps):
        return self.in_plane(steps), self.chip(PLANE if steps > 0 else -PLANE)

    def starts(self, steps, local):
        return jnp.logical_and(local == (PLANE - 1 if steps > 0 else 0), self.core == 1)

    def leaves(self, steps):
        return self.starts(steps, self.local)

    def hands_on(self, steps):
        return self.starts(steps, lax.rem(self.local - steps + PLANE, PLANE))

    def has_source(self, steps):
        return self.column != (0 if steps > 0 else TILE_COLS - 1)

    def has_target(self, steps):
        return self.column != (TILE_COLS - 1 if steps > 0 else 0)


def greet(place, extra=()):
    devices = [place.sibling(), place.chip(PLANE), place.chip(-PLANE), *extra]
    for sign in (1, -1):
        devices += [place.in_plane(sign)]
        devices += [place.chip(sign * steps) for steps in (1, TILE_COLS, TILE_COLS + 1)]
    barrier = pltpu.get_barrier_semaphore()
    for device in devices:
        pl.semaphore_signal(barrier, inc=1, device_id=device, device_id_type=MESH)
    pl.semaphore_wait(barrier, len(devices))


def halo_targets(i, j):
    targets = []
    if j == 0:
        targets.append((RIGHT + i, -1))
    if i == 0:
        targets.append((LOWER + j, -TILE_COLS))
    if i == 0 and j == 0:
        targets.append((DIAG, -TILE_COLS - 1))
    return targets


def remote(source, target, sems, at, device):
    return pltpu.make_async_remote_copy(
        src_ref=source,
        dst_ref=target,
        send_sem=sems.at[0, at],
        recv_sem=sems.at[1, at],
        device_id=device,
        device_id_type=MESH,
    )


class Routed:
    def __init__(self, place, steps, source, target, via, at, direct_sems, via_sems, on_sems):
        self.target = target
        self.direct = remote(source, target, direct_sems, at, place.chip(steps))
        self.sends = self.receives = True
        if abs(steps) == 1 or abs(steps) == TILE_COLS + 1:
            self.sends, self.receives = place.has_target(steps), place.has_source(steps)
        self.relayed = place.relayed(steps)
        if self.relayed:
            first, second = place.legs(steps)
            self.away = remote(source, via.at[at], via_sems, at, first)
            self.onward = pltpu.make_async_remote_copy(
                src_ref=via.at[at],
                dst_ref=target,
                send_sem=on_sems.at[at],
                recv_sem=direct_sems.at[1, at],
                device_id=second,
                device_id_type=MESH,
            )
            leaves = place.leaves(steps)
            self.leaves = jnp.logical_and(self.sends, leaves)
            self.stays = jnp.logical_and(self.sends, jnp.logical_not(leaves))
            self.hands_on = place.hands_on(steps)
        else:
            self.stays = self.sends

    def start(self):
        if self.relayed:
            pl.when(self.leaves)(self.away.start)
        pl.when(self.stays)(self.direct.start)

    def hand_on(self):
        if self.relayed:

            @pl.when(self.hands_on)
            def _():
                self.away.wait_recv()
                self.onward.start()

    def wait_recv(self):
        pl.when(self.receives)(self.direct.wait_recv)
        if self.receives is not True:

            @pl.when(jnp.logical_not(self.receives))
            def _():
                self.target[...] = jnp.zeros(self.target.shape, self.target.dtype)

    def wait_send(self):
        if self.relayed:
            pl.when(self.leaves)(self.away.wait_send)
            pl.when(self.hands_on)(self.onward.wait_send)
        pl.when(self.stays)(self.direct.wait_send)


def block_of(ref, channel, i, j, extent):
    return ref.at[channel, i * extent:(i + 1) * extent, j * extent:(j + 1) * extent]


HALO_ORDER = (RIGHT + 1, RIGHT, LOWER, DIAG, LOWER + 1)


def send_halos(place, copies, i, j, outgoing, halo, via, halo_sems, via_sems, on_sems):
    for piece, steps in halo_targets(i, j):
        copies[piece] = Routed(
            place, steps, outgoing.at[2 * i + j], halo.at[place.core, piece], via, piece,
            halo_sems, via_sems, on_sems,
        )
        copies[piece].start()


def pass_halos(place, halo, copies, pass_sems):
    passes = []
    for piece in HALO_ORDER:
        copies[piece].wait_recv()
        mine = halo.at[place.core, piece]
        passes.append(remote(mine, mine, pass_sems, piece, place.sibling()))
        passes[-1].start()
    for copy in passes:
        copy.wait()
    for copy in copies.values():
        copy.wait_send()


def first_halo_kernel(
    tile, halo, outgoing, via, halo_sems, via_sems, on_sems, pass_sems,
):
    place = Place()
    extent = outgoing.shape[-1]
    greet(place)
    copies = {}
    for i, j in ((0, 0), (1, 0), (0, 1)):
        outgoing[2 * i + j] = block_of(tile, place.core, i, j, extent)[...].astype(jnp.bfloat16)
        send_halos(place, copies, i, j, outgoing, halo, via, halo_sems, via_sems, on_sems)
    for piece in (RIGHT, RIGHT + 1, LOWER, LOWER + 1):
        copies[piece].hand_on()
    pass_halos(place, halo, copies, pass_sems)


def reduce_kernel(last, grads, tile, refined, *rest):
    if not last:
        halo, outgoing, halo_via, halo_sems, halo_via_sems, halo_on_sems, pass_sems = rest[:7]
        rest = rest[7:]
    (pair, edges, edges_in, edges_via, sums, sums_in, totals, totals_in,
     pair_sems, edge_sems, edge_via_sems, edge_on_sems,
     sum_sems, total_sems) = rest
    place = Place()
    extent = grads.shape[-1]
    core, other = place.core, place.other
    f32, bf16 = jnp.float32, jnp.bfloat16
    across = place.tiles
    greet(place, (place.chip(across),))
    margins = {5: (1, 1), 7: (3, TILE_COLS), 2: (0, 1), 8: (4, TILE_COLS + 1), 6: (2, TILE_COLS)}
    order = ((1, 1), (1, 0), (0, 0), (0, 1))
    needs = {(1, 1): (), (1, 0): (1,), (0, 0): (0, 2, 4), (0, 1): (3,)}
    pair_copies = {}
    for k in [4, *margins, 3, 0, 1]:
        pair_copies[k] = remote(grads.at[other, k], pair.at[k], pair_sems, k, place.sibling())
        pair_copies[k].start()
    edge_copies = {}
    sum_copies = {}
    under_way = []

    def send_sum(i, j):
        k = BAND * i + j
        at = 2 * i + j
        pair_copies[k].wait_recv()
        value = grads[core, k].astype(f32) + pair[k].astype(f32)
        for m in needs[i, j]:
            edge_copies[m].wait_recv()
            value = value + edges_in[m].astype(f32)
        sums[at] = value.astype(bf16)
        sum_copies[at] = remote(sums.at[at], sums_in.at[at], sum_sems, at, place.chip(across))
        if len(under_way) >= AHEAD:
            under_way.pop(0).wait_send()
        sum_copies[at].start()
        under_way.append(sum_copies[at])

    send_sum(1, 1)
    for k, (m, steps) in margins.items():
        pair_copies[k].wait_recv()
        edges[m] = (grads[core, k].astype(f32) + pair[k].astype(f32)).astype(bf16)
        edge_copies[m] = Routed(
            place, steps, edges.at[m], edges_in.at[m], edges_via, m,
            edge_sems, edge_via_sems, edge_on_sems,
        )
        edge_copies[m].start()
    edge_copies[1].hand_on()
    send_sum(1, 0)
    edge_copies[0].hand_on()
    for i, j in order[2:]:
        send_sum(i, j)

    total_copies = {}
    halo_copies = {}
    for i, j in order:
        at = 2 * i + j
        sum_copies[at].wait_recv()
        total = (sums[at].astype(f32) + sums_in[at].astype(f32)).astype(bf16)
        totals[at] = total
        total_copies[at] = remote(
            totals.at[at], totals_in.at[at], total_sems, at, place.sibling()
        )
        total_copies[at].start()
        fresh = block_of(tile, core, i, j, extent)[...] - LEARNING_RATE * total.astype(f32)
        block_of(refined, core, i, j, extent)[...] = fresh
        if not last and (i, j) != (1, 1):
            outgoing[at] = fresh.astype(bf16)
            send_halos(
                place, halo_copies, i, j, outgoing, halo, halo_via,
                halo_sems, halo_via_sems, halo_on_sems,
            )
            if (i, j) == (0, 0):
                for piece in (RIGHT + 1, LOWER, RIGHT):
                    halo_copies[piece].hand_on()
    if not last:
        halo_copies[LOWER + 1].hand_on()
    for i, j in order:
        at = 2 * i + j
        total_copies[at].wait_recv()
        block_of(refined, other, i, j, extent)[...] = block_of(tile, other, i, j, extent)[
            ...
        ] - LEARNING_RATE * totals_in[at].astype(f32)
    if not last:
        pass_halos(place, halo, halo_copies, pass_sems)
    for copy in (*pair_copies.values(), *edge_copies.values(), *under_way, *total_copies.values()):
        copy.wait_send()


def sems(count):
    return pltpu.SemaphoreType.DMA((2, count))


def first_halo(tile, extent):
    vmem = pl.BlockSpec(memory_space=pltpu.VMEM)
    return pl.pallas_call(
        first_halo_kernel,
        out_shape=jax.ShapeDtypeStruct((2, PIECES, extent, extent), jnp.bfloat16),
        in_specs=[vmem],
        out_specs=vmem,
        scratch_shapes=[
            pltpu.VMEM((4, extent, extent), jnp.bfloat16),
            pltpu.VMEM((PIECES, extent, extent), jnp.bfloat16),
            sems(PIECES),
            sems(PIECES),
            pltpu.SemaphoreType.DMA((PIECES,)),
            sems(PIECES),
        ],
        compiler_params=pltpu.CompilerParams(
            collective_id=0, has_side_effects=True, vmem_limit_bytes=40 * 1024 * 1024
        ),
    )(tile)


def reduce_and_update(grads, tile, last):
    extent = grads.shape[-1]
    vmem = pl.BlockSpec(memory_space=pltpu.VMEM)

    def blocks(count):
        return pltpu.VMEM((count, extent, extent), jnp.bfloat16)

    onward = pltpu.SemaphoreType.DMA((PIECES,))
    shapes = [jax.ShapeDtypeStruct(tile.shape, tile.dtype)]
    scratch = []
    if not last:
        shapes.append(jax.ShapeDtypeStruct((2, PIECES, extent, extent), jnp.bfloat16))
        scratch += [blocks(4), blocks(PIECES), sems(PIECES), sems(PIECES), onward, sems(PIECES)]
    scratch += [blocks(BAND * BAND), blocks(PIECES), blocks(PIECES), blocks(PIECES)]
    scratch += [blocks(4)] * 4
    scratch += [sems(BAND * BAND), sems(PIECES), sems(PIECES), onward]
    scratch += [sems(4), sems(4)]
    return pl.pallas_call(
        functools.partial(reduce_kernel, last),
        out_shape=tuple(shapes),
        in_specs=[vmem, vmem],
        out_specs=(vmem,) * len(shapes),
        scratch_shapes=scratch,
        compiler_params=pltpu.CompilerParams(
            collective_id=2 if last else 1,
            has_side_effects=True,
            vmem_limit_bytes=40 * 1024 * 1024,
        ),
    )(grads, tile)


def shards(object_tiles, probe, patterns, corners, counts):
    tile = object_tiles[0]
    extent = probe.shape[1]
    table, split = tables(extent)
    halo = first_halo(tile, extent)
    for repeat in range(ITERS):
        grads, *ordered = slot_gradients(
            tile, halo, probe, patterns, corners, counts, table, None if repeat else split
        )
        if ordered:
            patterns = ordered[0]
        tile, *rest = reduce_and_update(grads, tile, repeat == ITERS - 1)
        if rest:
            halo = rest[0]
    return tile[None]


def solution(mesh):
    return jax.shard_map(
        shards,
        mesh=mesh,
        in_specs=(
            P("tile", None, None, None),
            P(),
            P(("tile", "pos"), None, None),
            P(("tile", "pos"), None),
            P(("tile", "pos")),
        ),
        out_specs=P("tile", None, None, None),
        check_vma=False,
    )
```

```python
import functools
import math

import jax
import jax.numpy as jnp
import numpy as np
from jax import lax
from jax.experimental import pallas as pl
from jax.experimental.pallas import tpu as pltpu
from jax.sharding import PartitionSpec as P

TILE_COLS = 8
ITERS = 2
LEARNING_RATE = 0.03
LANES = 128
SUBLANES = 8
CHUNK = 32
GROUP = 16
BAND = 3
RIGHT, LOWER, DIAG, PIECES = 0, 2, 4, 5
PLANE = 16
LINE = 3
AHEAD = 2
MESH = pl.DeviceIdType.MESH


def tables(extent):
    counter = np.arange(extent, dtype=np.int64)
    phases = counter[:, None] * counter[None, :] % extent
    angles = phases.astype(np.float64) * (2.0 * math.pi / extent)
    factor = 1.0 / math.sqrt(extent)
    cosine = np.cos(angles) * factor
    sine_neg = -np.sin(angles) * factor
    matrices = []
    for parity in range(2):
        c = cosine[:extent // 2, parity::2]
        d = sine_neg[:extent // 2, parity::2]
        matrices.append(np.block([[c, d], [-d, c]]))
    matrices += [matrices[0].T, matrices[1].T]
    rows = np.arange(extent).reshape(2, -1, GROUP).swapaxes(0, 1).reshape(-1)
    matrices += [matrices[at][rows] for at in range(4)]
    order = np.concatenate([counter[0::2], counter[1::2]])
    split = (counter[:, None] == order[None, :]).astype(np.float32)
    return jnp.asarray(np.stack(matrices), jnp.bfloat16), jnp.asarray(
        np.stack([split, split.T]), jnp.bfloat16
    )


def slots_kernel(
    reorder, corners, counts, tile, halo, probe, patterns, table, *rest,
):
    if reorder:
        split, grad_blocks, ordered, *rest = rest
    else:
        grad_blocks, *rest = rest
        ordered = patterns
    image, grad, padded, rolled, wave, half = rest
    extent = probe.shape[1]
    edge = tile.shape[1]
    own = edge // LANES
    margin = extent // LANES
    mid_row = extent // 2
    f32 = jnp.float32
    for ch in range(2):
        for b in range(own):
            cols = slice(b * LANES, (b + 1) * LANES)
            image[b, ch, :edge] = tile[ch, :, cols]
            inner = slice(b % margin * LANES, (b % margin + 1) * LANES)
            image[b, ch, edge:] = halo[ch, LOWER + b // margin, :, inner].astype(f32)
        for b in range(margin):
            cols = slice(b * LANES, (b + 1) * LANES)
            for i in range(edge // extent):
                image[own + b, ch, i * extent:(i + 1) * extent] = halo[ch, RIGHT + i, :, cols].astype(f32)
            image[own + b, ch, edge:] = halo[ch, DIAG, :, cols].astype(f32)
            padded[ch, b, :SUBLANES] = probe[ch, extent - SUBLANES:, cols]
            padded[ch, b, SUBLANES:] = probe[ch, :, cols]
    grad[...] = jnp.zeros_like(grad)

    class Slot:
        def __init__(self, g, lane):
            self.g, self.lane = g, lane
            row, col = corners[g, 0], corners[g, 1]
            self.row_off = lax.rem(row, SUBLANES)
            self.col_off = lax.rem(col, LANES)
            self.row_at = pl.multiple_of(row - self.row_off, SUBLANES)
            self.block = lax.div(col, LANES)
            self.keep = lax.broadcasted_iota(jnp.int32, (CHUNK, LANES), 1) >= self.col_off
            self.keep8 = lax.broadcasted_iota(jnp.int32, (SUBLANES, LANES), 1) >= self.col_off
            self.stay8 = lax.broadcasted_iota(jnp.int32, (SUBLANES, LANES), 0) >= self.row_off
            self.below = pl.ds(pl.multiple_of(self.row_at + extent, SUBLANES), SUBLANES)

        def rows(self, i, number=CHUNK):
            return pl.ds(pl.multiple_of(self.row_at + i, SUBLANES), number)

        def illuminate(self):
            keep, keep8, stay8, block, lane = self.keep, self.keep8, self.stay8, self.block, self.lane
            for i in range(0, extent, CHUNK):
                here = slice(i, i + CHUNK)
                shifted = []
                for ch in range(2):
                    turned = [
                        pltpu.roll(
                            padded[ch, b, pl.ds(SUBLANES - self.row_off + i, CHUNK), :],
                            self.col_off, 1,
                        )
                        for b in range(2)
                    ]
                    shifted.append((
                        jnp.where(keep, turned[0], turned[1]), jnp.where(keep, turned[1], turned[0])
                    ))
                    rolled[lane, ch, 0, here] = shifted[ch][0]
                    rolled[lane, ch, 1, here] = shifted[ch][1]
                rows = self.rows(i)
                crops = []
                for ch in range(2):
                    left = jnp.where(
                        keep, image[block, ch, rows, :], image[block + 2, ch, rows, :]
                    )
                    mid = image[block + 1, ch, rows, :]
                    if i == 0:
                        below = self.below
                        left8 = jnp.where(
                            keep8, image[block, ch, below, :], image[block + 2, ch, below, :]
                        )
                        mid8 = image[block + 1, ch, below, :]
                        left = jnp.concatenate(
                            [jnp.where(stay8, left[:SUBLANES], left8), left[SUBLANES:]], 0
                        )
                        mid = jnp.concatenate(
                            [jnp.where(stay8, mid[:SUBLANES], mid8), mid[SUBLANES:]], 0
                        )
                    crops.append((left, mid))
                real = [
                    shifted[0][b] * crops[0][b] - shifted[1][b] * crops[1][b] for b in range(2)
                ]
                imag = [
                    shifted[0][b] * crops[1][b] + shifted[1][b] * crops[0][b] for b in range(2)
                ]
                wave[lane, 0, here, :LANES] = (real[0] + real[1]).astype(jnp.bfloat16)
                wave[lane, 0, here, LANES:] = (imag[0] + imag[1]).astype(jnp.bfloat16)
                wave[lane, 1, here, :LANES] = (real[0] - real[1]).astype(jnp.bfloat16)
                wave[lane, 1, here, LANES:] = (imag[0] - imag[1]).astype(jnp.bfloat16)

        def along_rows(self):
            lane = self.lane
            for q in range(2):
                freq = jnp.dot(wave[lane, q], table[q], preferred_element_type=f32)
                near, far = freq[:mid_row], freq[mid_row:]
                cols = slice(q * LANES, (q + 1) * LANES)
                for r, value in enumerate((near + far, near - far)):
                    half[lane, r, :mid_row, cols] = value[:, :LANES].astype(jnp.bfloat16)
                    half[lane, r, mid_row:, cols] = value[:, LANES:].astype(jnp.bfloat16)

        def along_columns(self, at, r):
            return jnp.dot(table[at + r], half[self.lane, r], preferred_element_type=f32)

        def push(self):
            lane = self.lane
            for r in range(2):
                freq = self.along_columns(6, r)
                for i in range(0, mid_row, GROUP):
                    here = slice(r * mid_row + i, r * mid_row + i + GROUP)
                    real = freq[2 * i:2 * i + GROUP]
                    imag = freq[2 * i + GROUP:2 * i + 2 * GROUP]
                    misfit = real * real + imag * imag - ordered[self.g, here].astype(f32)
                    real = (real * misfit).astype(jnp.bfloat16)
                    imag = (imag * misfit).astype(jnp.bfloat16)
                    for q in range(2):
                        cols = slice(q * LANES, (q + 1) * LANES)
                        wave[lane, q, here, :LANES] = real[:, cols]
                        wave[lane, q, here, LANES:] = imag[:, cols]

        def back_along_rows(self):
            lane = self.lane
            even = jnp.dot(wave[lane, 0], table[2], preferred_element_type=f32)
            odd = jnp.dot(wave[lane, 1], table[3], preferred_element_type=f32)
            for b, value in enumerate((even + odd, even - odd)):
                cols = slice(b * LANES, (b + 1) * LANES)
                for r in range(2):
                    rows = slice(r * mid_row, (r + 1) * mid_row)
                    half[lane, r, :mid_row, cols] = value[rows, :LANES].astype(jnp.bfloat16)
                    half[lane, r, mid_row:, cols] = value[rows, LANES:].astype(jnp.bfloat16)

        def gather(self):
            keep, keep8, stay8 = self.keep[:GROUP], self.keep8, self.stay8
            block, lane = self.block, self.lane
            even, odd = self.along_columns(4, 0), self.along_columns(4, 1)
            for i in range(0, extent, GROUP):
                here = slice(i, i + GROUP)
                rows = self.rows(i, GROUP)
                both = jnp.add if i < mid_row else jnp.subtract
                at = 2 * (i % mid_row)
                for b in range(2):
                    cols = slice(b * LANES, (b + 1) * LANES)
                    real = both(even[at:at + GROUP, cols], odd[at:at + GROUP, cols])
                    at_imag = slice(at + GROUP, at + 2 * GROUP)
                    imag = both(even[at_imag, cols], odd[at_imag, cols])
                    p_real = rolled[lane, 0, b, here]
                    p_imag = rolled[lane, 1, b, here]
                    parts = (p_real * real + p_imag * imag, p_real * imag - p_imag * real)
                    for ch in range(2):
                        value = parts[ch]
                        if i == 0:
                            spill = jnp.where(stay8, 0.0, value[:SUBLANES])
                            value = jnp.concatenate(
                                [jnp.where(stay8, value[:SUBLANES], 0.0), value[SUBLANES:]], 0
                            )
                            below = self.below
                            if b == 0:
                                grad[block, ch, below, :] += jnp.where(keep8, spill, 0.0)
                                grad[block + 2, ch, below, :] += jnp.where(keep8, 0.0, spill)
                            else:
                                grad[block + 1, ch, below, :] += spill
                        if b == 0:
                            grad[block, ch, rows, :] += jnp.where(keep, value, 0.0)
                            grad[block + 2, ch, rows, :] += jnp.where(keep, 0.0, value)
                        else:
                            grad[block + 1, ch, rows, :] += value

        def order(self):
            by_columns = jnp.dot(patterns[self.g], split[0], preferred_element_type=f32)
            by_rows = jnp.dot(
                split[1], by_columns.astype(jnp.bfloat16), preferred_element_type=f32
            )
            ordered[self.g] = by_rows.astype(jnp.bfloat16)

        def stages(self):
            return ((self.order,) if reorder else ()) + self.steps()

        def steps(self):
            return (
                self.illuminate,
                self.along_rows,
                self.push,
                self.back_along_rows,
                self.gather,
            )

    def pair(p, carry):
        ahead, behind = Slot(2 * p, 0).stages(), Slot(2 * p + 1, 1).stages()
        for a, b in zip(ahead, behind):
            a()
            b()
        return carry

    live = counts[0]
    lax.fori_loop(0, lax.div(live, 2), pair, 0)

    @pl.when(lax.rem(live, 2) == 1)
    def _():
        for stage in Slot(live - 1, 0).stages():
            stage()

    for ch in range(2):
        for i in range(BAND):
            rows = slice(i * extent, (i + 1) * extent)
            for b in range(BAND * margin):
                cols = slice(b % margin * LANES, (b % margin + 1) * LANES)
                grad_blocks[ch, i * BAND + b // margin, :, cols] = grad[b, ch, rows].astype(
                    jnp.bfloat16
                )


def slot_gradients(tile, halo, probe, patterns, corners, counts, table, split=None):
    extent = probe.shape[1]
    edge = tile.shape[1]
    total = edge + extent
    blocks = total // LANES
    f32, bf16 = jnp.float32, jnp.bfloat16
    vmem = pl.BlockSpec(memory_space=pltpu.VMEM)
    smem = pl.BlockSpec(memory_space=pltpu.SMEM)
    reorder = split is not None
    shapes = [jax.ShapeDtypeStruct((2, BAND * BAND, extent, extent), bf16)]
    operands = [corners, counts, tile, halo, probe, patterns, table]
    if reorder:
        shapes.append(jax.ShapeDtypeStruct(patterns.shape, patterns.dtype))
        operands.append(split)
    return pl.pallas_call(
        functools.partial(slots_kernel, reorder),
        out_shape=tuple(shapes),
        in_specs=[smem, smem] + [vmem] * (len(operands) - 2),
        out_specs=(vmem,) * len(shapes),
        scratch_shapes=[
            pltpu.VMEM((blocks, 2, total, LANES), f32),
            pltpu.VMEM((blocks, 2, total, LANES), f32),
            pltpu.VMEM((2, 2, extent + SUBLANES, LANES), f32),
            pltpu.VMEM((2, 2, 2, extent, LANES), f32),
            pltpu.VMEM((2, 2, extent, extent), bf16),
            pltpu.VMEM((2, 2, extent, extent), bf16),
        ],
        compiler_params=pltpu.CompilerParams(vmem_limit_bytes=40 * 1024 * 1024),
        cost_estimate=pl.CostEstimate(
            flops=4 * 4 * 2 * extent**3 * 2, bytes_accessed=8 * 2**20, transcendentals=0
        ),
    )(*operands)


class Place:
    def __init__(self):
        self.tiles = lax.axis_size("tile")
        self.chips = self.tiles * (lax.axis_size("pos") // 2)
        pos = lax.axis_index("pos")
        self.core = lax.rem(pos, 2)
        self.other = 1 - self.core
        self.flat = lax.div(pos, 2) * self.tiles + lax.axis_index("tile")
        self.local = lax.rem(self.flat, PLANE)
        self.column = lax.rem(self.flat + TILE_COLS + TILE_COLS // 2, TILE_COLS)

    def at(self, flat, core):
        return lax.rem(flat, self.tiles), lax.div(flat, self.tiles) * 2 + core

    def device(self, steps, core):
        return self.at(lax.rem(self.flat + steps + self.chips, self.chips), core)

    def sibling(self):
        return self.device(0, self.other)

    def chip(self, steps):
        return self.device(steps, self.core)

    def in_plane(self, steps):
        local = lax.rem(self.local + steps + PLANE, PLANE)
        return self.at(self.flat - self.local + local, self.core)

    def relayed(self, steps):
        return abs(steps) == 1

    def legs(self, steps):
        if steps > 0:
            return self.in_plane(steps), self.chip(PLANE)
        over = jnp.logical_and(self.local == 0, self.core == 1)
        onward = jnp.where(self.local == PLANE - 1, -PLANE, -1 - LINE)
        return self.chip(jnp.where(over, PLANE - 1, LINE)), self.chip(onward)

    def leaves(self, steps):
        if steps > 0:
            return jnp.logical_and(self.local == PLANE - 1, self.core == 1)
        middle = jnp.logical_and(self.local == TILE_COLS, self.core == 1)
        return jnp.logical_or(self.local == 0, middle)

    def hands_on(self, steps):
        if steps > 0:
            return jnp.logical_and(self.local == 0, self.core == 1)
        far = jnp.logical_or(self.local == PLANE - 1, self.local == TILE_COLS + LINE)
        return jnp.logical_or(
            jnp.logical_and(far, self.core == 1),
            jnp.logical_and(self.local == LINE, self.core == 0),
        )

    def has_source(self, steps):
        return self.column != (0 if steps > 0 else TILE_COLS - 1)

    def has_target(self, steps):
        return self.column != (TILE_COLS - 1 if steps > 0 else 0)


def greet(place, halos, extra=()):
    devices = [place.sibling(), place.chip(PLANE), place.chip(-PLANE), *extra]
    for sign in (1, -1):
        devices += [place.in_plane(sign)]
        devices += [place.chip(sign * steps) for steps in (1, TILE_COLS, TILE_COLS + 1)]
        if halos:
            devices += [place.chip(sign * LINE), place.chip(sign * (LINE + 1))]
    barrier = pltpu.get_barrier_semaphore()
    for device in devices:
        pl.semaphore_signal(barrier, inc=1, device_id=device, device_id_type=MESH)
    pl.semaphore_wait(barrier, len(devices))


def halo_targets(i, j):
    targets = []
    if j == 0:
        targets.append((RIGHT + i, -1))
    if i == 0:
        targets.append((LOWER + j, -TILE_COLS))
    if i == 0 and j == 0:
        targets.append((DIAG, -TILE_COLS - 1))
    return targets


def remote(source, target, sems, at, device):
    return pltpu.make_async_remote_copy(
        src_ref=source,
        dst_ref=target,
        send_sem=sems.at[0, at],
        recv_sem=sems.at[1, at],
        device_id=device,
        device_id_type=MESH,
    )


class Routed:
    def __init__(self, place, steps, source, target, via, at, direct_sems, via_sems, on_sems):
        self.target = target
        self.direct = remote(source, target, direct_sems, at, place.chip(steps))
        self.sends = self.receives = True
        if abs(steps) == 1 or abs(steps) == TILE_COLS + 1:
            self.sends, self.receives = place.has_target(steps), place.has_source(steps)
        self.relayed = place.relayed(steps)
        if self.relayed:
            first, second = place.legs(steps)
            self.away = remote(source, via.at[at], via_sems, at, first)
            self.onward = pltpu.make_async_remote_copy(
                src_ref=via.at[at],
                dst_ref=target,
                send_sem=on_sems.at[at],
                recv_sem=direct_sems.at[1, at],
                device_id=second,
                device_id_type=MESH,
            )
            leaves = place.leaves(steps)
            self.leaves = jnp.logical_and(self.sends, leaves)
            self.stays = jnp.logical_and(self.sends, jnp.logical_not(leaves))
            self.hands_on = place.hands_on(steps)
        else:
            self.stays = self.sends

    def start(self):
        if self.relayed:
            pl.when(self.leaves)(self.away.start)
        pl.when(self.stays)(self.direct.start)

    def hand_on(self):
        if self.relayed:

            @pl.when(self.hands_on)
            def _():
                self.away.wait_recv()
                self.onward.start()

    def wait_recv(self):
        pl.when(self.receives)(self.direct.wait_recv)
        if self.receives is not True:

            @pl.when(jnp.logical_not(self.receives))
            def _():
                self.target[...] = jnp.zeros(self.target.shape, self.target.dtype)

    def wait_send(self):
        if self.relayed:
            pl.when(self.leaves)(self.away.wait_send)
            pl.when(self.hands_on)(self.onward.wait_send)
        pl.when(self.stays)(self.direct.wait_send)


def block_of(ref, channel, i, j, extent):
    return ref.at[channel, i * extent:(i + 1) * extent, j * extent:(j + 1) * extent]


HALO_ORDER = (RIGHT + 1, RIGHT, LOWER, DIAG, LOWER + 1)


def send_halos(place, copies, i, j, outgoing, halo, via, halo_sems, via_sems, on_sems):
    for piece, steps in halo_targets(i, j):
        copies[piece] = Routed(
            place, steps, outgoing.at[2 * i + j], halo.at[place.core, piece], via, piece,
            halo_sems, via_sems, on_sems,
        )
        copies[piece].start()


def pass_halos(place, halo, copies, pass_sems):
    passes = []
    for piece in HALO_ORDER:
        copies[piece].wait_recv()
        mine = halo.at[place.core, piece]
        passes.append(remote(mine, mine, pass_sems, piece, place.sibling()))
        passes[-1].start()
    for copy in passes:
        copy.wait()
    for copy in copies.values():
        copy.wait_send()


def first_halo_kernel(
    tile, halo, outgoing, via, halo_sems, via_sems, on_sems, pass_sems,
):
    place = Place()
    extent = outgoing.shape[-1]
    greet(place, True)
    copies = {}
    for i, j in ((0, 0), (1, 0), (0, 1)):
        outgoing[2 * i + j] = block_of(tile, place.core, i, j, extent)[...].astype(jnp.bfloat16)
        send_halos(place, copies, i, j, outgoing, halo, via, halo_sems, via_sems, on_sems)
    for piece in (RIGHT, RIGHT + 1, LOWER, LOWER + 1):
        copies[piece].hand_on()
    pass_halos(place, halo, copies, pass_sems)


def reduce_kernel(last, grads, tile, refined, *rest):
    if not last:
        halo, outgoing, halo_via, halo_sems, halo_via_sems, halo_on_sems, pass_sems = rest[:7]
        rest = rest[7:]
    (pair, edges, edges_in, edges_via, sums, sums_in, totals, totals_in,
     pair_sems, edge_sems, edge_via_sems, edge_on_sems,
     sum_sems, total_sems) = rest
    place = Place()
    extent = grads.shape[-1]
    core, other = place.core, place.other
    f32, bf16 = jnp.float32, jnp.bfloat16
    across = place.tiles
    greet(place, not last, (place.chip(across),))
    margins = {5: (1, 1), 7: (3, TILE_COLS), 2: (0, 1), 8: (4, TILE_COLS + 1), 6: (2, TILE_COLS)}
    order = ((1, 1), (1, 0), (0, 0), (0, 1))
    needs = {(1, 1): (), (1, 0): (1,), (0, 0): (0, 2, 4), (0, 1): (3,)}
    pair_copies = {}
    for k in [4, *margins, 3, 0, 1]:
        pair_copies[k] = remote(grads.at[other, k], pair.at[k], pair_sems, k, place.sibling())
        pair_copies[k].start()
    edge_copies = {}
    sum_copies = {}
    under_way = []

    def send_sum(i, j):
        k = BAND * i + j
        at = 2 * i + j
        pair_copies[k].wait_recv()
        value = grads[core, k].astype(f32) + pair[k].astype(f32)
        for m in needs[i, j]:
            edge_copies[m].wait_recv()
            value = value + edges_in[m].astype(f32)
        sums[at] = value.astype(bf16)
        sum_copies[at] = remote(sums.at[at], sums_in.at[at], sum_sems, at, place.chip(across))
        if len(under_way) >= AHEAD:
            under_way.pop(0).wait_send()
        sum_copies[at].start()
        under_way.append(sum_copies[at])

    send_sum(1, 1)
    for k, (m, steps) in margins.items():
        pair_copies[k].wait_recv()
        edges[m] = (grads[core, k].astype(f32) + pair[k].astype(f32)).astype(bf16)
        edge_copies[m] = Routed(
            place, steps, edges.at[m], edges_in.at[m], edges_via, m,
            edge_sems, edge_via_sems, edge_on_sems,
        )
        edge_copies[m].start()
    edge_copies[1].hand_on()
    send_sum(1, 0)
    edge_copies[0].hand_on()
    for i, j in order[2:]:
        send_sum(i, j)

    total_copies = {}
    halo_copies = {}
    for i, j in order:
        at = 2 * i + j
        sum_copies[at].wait_recv()
        total = (sums[at].astype(f32) + sums_in[at].astype(f32)).astype(bf16)
        totals[at] = total
        total_copies[at] = remote(
            totals.at[at], totals_in.at[at], total_sems, at, place.sibling()
        )
        total_copies[at].start()
        fresh = block_of(tile, core, i, j, extent)[...] - LEARNING_RATE * total.astype(f32)
        block_of(refined, core, i, j, extent)[...] = fresh
        if not last and (i, j) != (1, 1):
            outgoing[at] = fresh.astype(bf16)
            send_halos(
                place, halo_copies, i, j, outgoing, halo, halo_via,
                halo_sems, halo_via_sems, halo_on_sems,
            )
            if (i, j) == (0, 0):
                for piece in (RIGHT + 1, LOWER, RIGHT):
                    halo_copies[piece].hand_on()
    if not last:
        halo_copies[LOWER + 1].hand_on()
    for i, j in order:
        at = 2 * i + j
        total_copies[at].wait_recv()
        block_of(refined, other, i, j, extent)[...] = block_of(tile, other, i, j, extent)[
            ...
        ] - LEARNING_RATE * totals_in[at].astype(f32)
    if not last:
        pass_halos(place, halo, halo_copies, pass_sems)
    for copy in (*pair_copies.values(), *edge_copies.values(), *under_way, *total_copies.values()):
        copy.wait_send()


def sems(count):
    return pltpu.SemaphoreType.DMA((2, count))


def first_halo(tile, extent):
    vmem = pl.BlockSpec(memory_space=pltpu.VMEM)
    return pl.pallas_call(
        first_halo_kernel,
        out_shape=jax.ShapeDtypeStruct((2, PIECES, extent, extent), jnp.bfloat16),
        in_specs=[vmem],
        out_specs=vmem,
        scratch_shapes=[
            pltpu.VMEM((4, extent, extent), jnp.bfloat16),
            pltpu.VMEM((PIECES, extent, extent), jnp.bfloat16),
            sems(PIECES),
            sems(PIECES),
            pltpu.SemaphoreType.DMA((PIECES,)),
            sems(PIECES),
        ],
        compiler_params=pltpu.CompilerParams(
            collective_id=0, has_side_effects=True, vmem_limit_bytes=40 * 1024 * 1024
        ),
    )(tile)


def reduce_and_update(grads, tile, last):
    extent = grads.shape[-1]
    vmem = pl.BlockSpec(memory_space=pltpu.VMEM)

    def blocks(count):
        return pltpu.VMEM((count, extent, extent), jnp.bfloat16)

    onward = pltpu.SemaphoreType.DMA((PIECES,))
    shapes = [jax.ShapeDtypeStruct(tile.shape, tile.dtype)]
    scratch = []
    if not last:
        shapes.append(jax.ShapeDtypeStruct((2, PIECES, extent, extent), jnp.bfloat16))
        scratch += [blocks(4), blocks(PIECES), sems(PIECES), sems(PIECES), onward, sems(PIECES)]
    scratch += [blocks(BAND * BAND), blocks(PIECES), blocks(PIECES), blocks(PIECES)]
    scratch += [blocks(4)] * 4
    scratch += [sems(BAND * BAND), sems(PIECES), sems(PIECES), onward]
    scratch += [sems(4), sems(4)]
    return pl.pallas_call(
        functools.partial(reduce_kernel, last),
        out_shape=tuple(shapes),
        in_specs=[vmem, vmem],
        out_specs=(vmem,) * len(shapes),
        scratch_shapes=scratch,
        compiler_params=pltpu.CompilerParams(
            collective_id=2 if last else 1,
            has_side_effects=True,
            vmem_limit_bytes=40 * 1024 * 1024,
        ),
    )(grads, tile)


def shards(object_tiles, probe, patterns, corners, counts):
    tile = object_tiles[0]
    extent = probe.shape[1]
    table, split = tables(extent)
    halo = first_halo(tile, extent)
    for repeat in range(ITERS):
        grads, *ordered = slot_gradients(
            tile, halo, probe, patterns, corners, counts, table, None if repeat else split
        )
        if ordered:
            patterns = ordered[0]
        tile, *rest = reduce_and_update(grads, tile, repeat == ITERS - 1)
        if rest:
            halo = rest[0]
    return tile[None]


def solution(mesh):
    return jax.shard_map(
        shards,
        mesh=mesh,
        in_specs=(
            P("tile", None, None, None),
            P(),
            P(("tile", "pos"), None, None),
            P(("tile", "pos"), None),
            P(("tile", "pos")),
        ),
        out_specs=P("tile", None, None, None),
        check_vma=False,
    )
```
